32 devices in a mesh: rep: 4 (over y, x), grp: 8 (over z, core).
Axes of the slice: x: 2, y: 2, z: 4, core: 2. Of those that a mesh axis runs over, the one named last changes fastest.
Arguments:
- activations: bfloat16 [16384, 512], P(('rep', 'grp')), may hold values from -6 to 6
- out_grads: bfloat16 [16384, 1024], P(('rep', 'grp')), may hold values from -0.00390625 to 0.00390625
- stats_old: float32 [4, 512, 512], P(None, 'grp'), as said below
Outputs:
- stats_new: float32 [4, 512, 512], P(None, 'grp')
- update: float32 [2, 512, 512], P(None, 'grp')
The draws below stay inside these ranges and needn't reach their ends.
Inputs may be any that keep to these rules, and one draw needn't show every extreme that they name: Each stats_old[c] is symmetric positive definite.
All inputs are finite; a program needn't handle non-finite values.
Results may differ from the reference program's by a relative error of at most 0.0009.
The reference program's roundings to bfloat16 on the way count: a program that leaves them out, or rounds other values in their place, can miss the bound.
Values may be sent and summed in bfloat16 or wider, within the bound.
No kernel may reach another device: no remote copies, remote signals or barrier semaphores. Data moves between devices by JAX's collectives and lax.ppermute only.
A program may use at most 64 MiB of HBM per device.

```python
import math
import jax
import jax.numpy as jnp
from jax import lax

BLK = 512
TILES = 2
ITERS = 2
TOKENS = 16384


def draw_stats_old(key, part):
    key_base = jax.random.fold_in(key, 11)
    key_jitter = jax.random.fold_in(key, 12)
    base = jax.random.normal(key_base, (2 * TILES, BLK, BLK), jnp.float32)
    spread = math.log(3.0)
    gram = jnp.einsum('cij,ckj->cik', base, base) / BLK + jnp.eye(BLK, dtype=jnp.float32)
    jitter = jax.random.uniform(key_jitter, (2 * TILES, BLK), jnp.float32, -0.35, 0.35)
    rising = jnp.arange(BLK, dtype=jnp.float32) / BLK * spread
    scales = jnp.exp(rising[None, :] + jitter)
    return gram * scales[:, :, None] * scales[:, None, :]


def spiked(values, key, source, target, shards_of, factor):
    def block_of(dim):
        return (jnp.arange(values.shape[dim]) // (values.shape[dim] // shards_of)).reshape((-1,) + (1,) * (values.ndim - 1 - dim))

    near = jax.random.permutation(key, shards_of)[block_of(target)]
    second = (block_of(target) + shards_of // 2) % shards_of
    return jnp.where((block_of(source) == near) | (block_of(source) == second), factor * values, values)


def block_scale(rng, dims, shards, least, largest):
    gain = 1.0
    for axis_at, parts in shards:
        draws = jax.random.uniform(jax.random.fold_in(jax.random.fold_in(rng, 6), axis_at), (parts,), jnp.float32, least / len(shards), largest / len(shards))
        gain = gain * jnp.repeat(jnp.exp(draws), dims[axis_at] // parts).reshape((-1,) + (1,) * (len(dims) - 1 - axis_at))
    return gain


def scatter_about(stream_key, shape, width, most, cuts=(), kind=jnp.bfloat16):
    loudness = block_scale(stream_key, shape, cuts, -0.22, 0.18) if cuts else 1.0
    array = jax.random.normal(stream_key, shape, jnp.float32) * width * loudness
    return jnp.minimum(jnp.maximum(array, -most), most).astype(kind)


def gaussian_with(key, dims, scale, most, split, heavy, kind=jnp.bfloat16):
    result = scale * jax.random.normal(key, dims, jnp.float32)
    if split:
        result = result * block_scale(key, dims, split, -0.22, 0.18)
    return jnp.clip(spiked(result, jax.random.fold_in(key, 3), *heavy), -most, most).astype(kind)


def setup_inputs(seed: int = 0) -> dict:
    arg_keys = jax.random.split(jax.random.key(seed), 4)
    return {
        "activations": scatter_about(arg_keys[0], (TOKENS, BLK), 1.0, 6.0, ((0, 32),)),
        "out_grads": gaussian_with(arg_keys[1], (TOKENS, TILES * BLK), (TOKENS * BLK) ** -0.5, 0.00390625, ((0, 32),), (0, 1, 32, 2.75)),
        "stats_old": draw_stats_old(jax.random.fold_in(arg_keys[3], 71), 0),
    }


DAMPING = 0.01

def newton_root(damped):
    order_size = damped.shape[0]
    identity = jnp.eye(order_size, dtype=jnp.float32)
    scale = 2.5 / jnp.sqrt(jnp.sum(damped * damped))
    iterate = scale * damped
    factors = []
    for iteration in range(ITERS):
        factor = ((5.0 * identity - iterate) * 0.25).astype(jnp.bfloat16)
        factors.append(factor)
        if iteration + 1 < ITERS:
            upcast = factor.astype(jnp.float32)
            for repeat in range(4):
                iterate = jnp.dot(iterate, upcast, precision=lax.Precision.HIGHEST)
    if len(factors) == 1:
        running = factors[0].astype(jnp.float32)
    else:
        running = jnp.dot(factors[0], factors[1], preferred_element_type=jnp.float32)
        for later in factors[2:]:
            running = jnp.dot(running, later.astype(jnp.float32), precision=lax.Precision.HIGHEST)
    return (scale ** 0.25 * running).astype(jnp.bfloat16)

def reference(activations, out_grads, stats_old):
    token_total = activations.shape[0]
    block_rows = math.gcd(token_total, 4096)
    block_count = token_total // block_rows

    def accumulate(carry, index):
        first_row = (index * block_rows).astype(jnp.int32)
        inputs = lax.dynamic_slice_in_dim(activations, first_row, block_rows, 0)
        grads = lax.dynamic_slice_in_dim(out_grads, first_row, block_rows, 0)
        return (carry + jnp.dot(grads.T, inputs, preferred_element_type=jnp.float32), None)
    summed, _ = lax.scan(accumulate, jnp.zeros((TILES * BLK, BLK), jnp.float32), jnp.arange(block_count, dtype=jnp.int32))
    gradient = summed.astype(jnp.bfloat16).reshape(TILES, BLK, BLK)
    left_terms = [jnp.dot(gradient[tile].T, gradient[tile], preferred_element_type=jnp.float32) for tile in range(TILES)]
    right_terms = [jnp.dot(gradient[tile], gradient[tile].T, preferred_element_type=jnp.float32) for tile in range(TILES)]
    stats_new = stats_old + jnp.stack(left_terms + right_terms)
    identity = jnp.eye(BLK, dtype=jnp.float32)
    roots = [newton_root(stats_new[chain] + DAMPING * identity) for chain in range(2 * TILES)]
    updates = []
    for tile in range(TILES):
        inner_rows = jnp.dot(roots[TILES + tile], gradient[tile], preferred_element_type=jnp.float32)
        updates.append(jnp.dot(inner_rows, roots[tile].astype(jnp.float32), precision=lax.Precision.HIGHEST) * math.sqrt(BLK))
    return (stats_new, jnp.stack(updates))
```

```python
import functools
import math

import jax
import jax.numpy as jnp
from jax import lax
from jax.experimental import pallas as pl
from jax.experimental.pallas import tpu as pltpu
from jax.sharding import PartitionSpec as P

F32 = jnp.float32
BF16 = jnp.bfloat16
DAMPING = 0.01
TILE = 16
RADIX = 4


def swap(array, axis, mask):
    size = lax.axis_size(axis)
    return lax.ppermute(array, axis, [(i, i ^ mask) for i in range(size)])


def plan(axis, low, size, rows):
    steps = []
    shift, left = low + size.bit_length() - 1, size
    while left > 1:
        radix = min(RADIX, left)
        splits = rows // radix >= TILE and rows % radix == 0
        if not splits:
            radix = 2
        shift -= radix.bit_length() - 1
        left //= radix
        rows = rows // radix if splits else rows
        steps.append((axis, shift, radix, splits))
    return steps, rows


def vmem(count):
    return [pl.BlockSpec(memory_space=pltpu.VMEM)] * count


SMEM = pl.BlockSpec(memory_space=pltpu.SMEM)


def dot(a, b, contract=(1, 0)):
    return lax.dot_general(
        a, b, (((contract[0],), (contract[1],)), ((), ())), preferred_element_type=F32
    )


def term_kernel(place, grads, acts, out, *, other, rows):
    order = acts.shape[1]
    tile = place[0] ^ other
    columns = pl.ds(pl.multiple_of(tile * order, order), order)
    term = dot(grads[:, columns], acts[...], (0, 0))
    for block in range(order // rows):
        start = pl.multiple_of((block ^ place[1]) * rows, rows)
        out[pl.ds(start, rows), :] = term[block * rows : (block + 1) * rows]


def gradient_term(place, grads, acts, other, rows):
    tokens, order = acts.shape
    return pl.pallas_call(
        functools.partial(term_kernel, other=other, rows=rows),
        out_shape=jax.ShapeDtypeStruct((order, order), F32),
        in_specs=[SMEM] + vmem(2),
        out_specs=vmem(1)[0],
        compiler_params=pltpu.CompilerParams(vmem_limit_bytes=16 << 20),
        cost_estimate=pl.CostEstimate(
            flops=2 * tokens * order * order, bytes_accessed=4 * tokens * order, transcendentals=0
        ),
        name="gradient_term",
    )(place, grads, acts)


def on_diagonal(rows, columns, start):
    row = lax.broadcasted_iota(jnp.int32, (rows, columns), 0) + start
    return lax.broadcasted_iota(jnp.int32, (rows, columns), 1) == row


def pack_kernel(place, stats, keep, send, *, tiles):
    rows, order = stats.shape[1:]
    diagonal = on_diagonal(rows, order, place[3])
    for out, other in ((keep, 0), (send, 1)):
        extra = []
        for side in range(2):
            values = stats[side * tiles + (place[0] ^ other)]
            high = values.astype(BF16)
            out[side * rows : (side + 1) * rows, :] = high
            rest = values - high.astype(F32)
            rest = jnp.sum(jnp.where(diagonal, rest, 0.0), axis=0, keepdims=True)
            middle = rest.astype(BF16).astype(F32)
            extra += [middle, rest - middle]
        row = lax.broadcasted_iota(jnp.int32, (TILE, order), 0)
        tail = jnp.zeros((TILE, order), F32)
        for index, vector in enumerate(extra):
            tail = jnp.where(row == index, vector, tail)
        out[2 * rows :, :] = tail.astype(BF16)


def unpack_kernel(place, *refs, rows):
    parts, out = refs[:-1], refs[-1]
    order = out.shape[2]
    height = 2 * rows + TILE
    vectors = [jnp.full((1, order), DAMPING, F32) for _ in range(2)]
    for part in parts:
        for core in range(2):
            tail = part[core * height + 2 * rows : (core + 1) * height, :].astype(F32)
            for side in range(2):
                vectors[side] += tail[2 * side : 2 * side + 1] + tail[2 * side + 1 : 2 * side + 2]
    for index, part in enumerate(parts):
        for core in range(2):
            start = ((place[2] ^ index) * 2 + (place[0] ^ core)) * rows
            start = pl.multiple_of(start, rows)
            diagonal = on_diagonal(rows, order, start)
            for side in range(2):
                low = core * height + side * rows
                values = part[low : low + rows, :].astype(F32)
                out[side, pl.ds(start, rows), :] = values + jnp.where(diagonal, vectors[side], 0.0)


def step_kernel(place, damped, *refs, pieces, rows, band):
    parts = refs[:pieces]
    own, sent, grad, gram, scaled, power, factors, offs, seconds, left_root, right_rows = refs[pieces:]
    order = grad.shape[0]
    for index, part in enumerate(parts):
        for low in range(0, part.shape[0], rows):
            block = (index * part.shape[0] + low) // rows
            start = pl.multiple_of((block ^ place[1]) * rows, rows)
            grad[pl.ds(start, rows), :] = part[low : low + rows, :]
    row_own = pl.ds(pl.multiple_of(place[3], band), band)
    row_sent = pl.ds(pl.multiple_of(place[4], band), band)
    step = min(order, 256)
    strips = [slice(low, low + step) for low in range(0, order, step)]
    eyes = [on_diagonal(step, order, low) for low in range(0, order, step)]
    sides = range(2)
    sums = [jnp.zeros((1, 1), F32) for _ in sides]
    for side in sides:
        gram[side] = dot(grad[...], grad[...], (side, side))
        for strip in strips:
            damp = gram[side, strip, :] + damped[side, strip, :]
            scaled[side, strip, :] = damp
            sums[side] += jnp.sum(damp * damp, keepdims=True)
        own[side] = gram[side, row_own, :]
        sent[side] = gram[side, row_sent, :]
    scales = [2.5 / jnp.sqrt(total) for total in sums]
    for side in sides:
        for strip, eye in zip(strips, eyes):
            iterate = scaled[side, strip, :] * scales[side]
            scaled[side, strip, :] = iterate
            factor = ((jnp.where(eye, 5.0, 0.0) - iterate) * 0.25).astype(BF16)
            factors[side, strip, :] = factor
            offs[side, strip, :] = (factor.astype(F32) - jnp.where(eye, 1.25, 0.0)).astype(BF16)
    across = [jnp.zeros((1, order), F32) for _ in sides]
    for side in sides:
        power[side] = dot(offs[side], offs[side])
        for strip, eye in zip(strips, eyes):
            value = power[side, strip, :] + 2.5 * offs[side, strip, :].astype(F32)
            power[side, strip, :] = value
            across[side] += jnp.sum(jnp.where(eye, value, 0.0), axis=0, keepdims=True)
            seconds[side, strip, :] = jnp.where(eye, 0.0, value).astype(BF16)
    beside = [jnp.zeros((1, order), F32) for _ in sides]
    for side in sides:
        gram[side] = dot(seconds[side], seconds[side])
        for strip, eye in zip(strips, eyes):
            value = power[side, strip, :]
            down = jnp.sum(jnp.where(eye, value, 0.0), axis=1, keepdims=True)
            value = gram[side, strip, :] + value * (3.125 + down + across[side]) - jnp.where(eye, down * down, 0.0)
            power[side, strip, :] = value
            beside[side] += jnp.sum(jnp.where(eye, value, 0.0), axis=0, keepdims=True)
            offs[side, strip, :] = jnp.where(eye, 0.0, value).astype(BF16)
            seconds[side, strip, :] = jnp.where(eye, 0.0, scaled[side, strip, :]).astype(BF16)
    for side in sides:
        gram[side] = dot(seconds[side], offs[side])
        for strip, eye in zip(strips, eyes):
            first, value = scaled[side, strip, :], power[side, strip, :]
            down = jnp.sum(jnp.where(eye, first, 0.0), axis=1, keepdims=True)
            iterate = gram[side, strip, :] + 2.44140625 * first + down * value
            iterate += jnp.where(eye, 0.0, first) * beside[side]
            factor = ((jnp.where(eye, 5.0, 0.0) - iterate) * 0.25).astype(BF16)
            offs[side, strip, :] = factor
    quarters = [jnp.sqrt(jnp.sqrt(scale)) for scale in scales]
    left_root[...] = (dot(factors[0], offs[0]) * quarters[0]).astype(BF16)
    right_rows[:band] = factors[1, row_own, :]
    right_rows[band:] = factors[1, row_sent, :]
    right_root = (dot(right_rows[...], offs[1]) * quarters[1]).astype(BF16)
    inner = dot(right_root, grad[...])
    high = inner.astype(BF16)
    low = (inner - high.astype(F32)).astype(BF16)
    update = (dot(high, left_root[...]) + dot(low, left_root[...])) * math.sqrt(order)
    own[2] = update[:band]
    sent[2] = update[band:]


def on_device(activations, out_grads, stats_old):
    order = activations.shape[1]
    tiles = out_grads.shape[1] // order
    band = stats_old.shape[1]
    rep, grp = lax.axis_index("rep"), lax.axis_index("grp")
    reps, lines = lax.axis_size("rep"), lax.axis_size("grp") // 2
    core, line = grp & 1, grp >> 1

    across, rows = plan("rep", 0, reps, order)
    along, rows = plan("grp", 1, lines, rows)
    steps = across + along
    here = jnp.int32(0)
    for axis, shift, radix, splits in steps:
        if splits:
            here = here * radix + ((lax.axis_index(axis) >> shift) & (radix - 1))
    place = jnp.stack([core, here, line, grp * band, (grp ^ 1) * band]).astype(jnp.int32)

    sent = gradient_term(place, out_grads, activations, 1, rows)
    sent = swap(sent, "grp", 1)
    total = gradient_term(place, out_grads, activations, 0, rows)

    packed = jax.ShapeDtypeStruct((2 * band + TILE, order), BF16)
    keep, send = pl.pallas_call(
        functools.partial(pack_kernel, tiles=tiles),
        out_shape=(packed, packed),
        in_specs=[SMEM] + vmem(1),
        out_specs=tuple(vmem(2)),
        compiler_params=pltpu.CompilerParams(vmem_limit_bytes=8 << 20),
        cost_estimate=pl.CostEstimate(flops=band * order * 20, bytes_accessed=band * order * 32, transcendentals=0),
        name="pack_stats",
    )(place, stats_old)
    packed = jnp.concatenate([keep, swap(send, "grp", 1)], axis=0)

    total = total + sent
    for axis, shift, radix, splits in across + along:
        if splits:
            total = total.reshape(radix, -1, order)
            parts = [swap(total[digit], axis, digit << shift) for digit in range(1, radix)]
            total = sum(parts, total[0])
        else:
            total = total + swap(total, axis, 1 << shift)
    stats = [packed]
    for digit in range(1, lines):
        stats.append(swap(packed, "grp", digit << 1))
    damped = pl.pallas_call(
        functools.partial(unpack_kernel, rows=band),
        out_shape=jax.ShapeDtypeStruct((2, order, order), F32),
        in_specs=[SMEM] + vmem(len(stats)),
        out_specs=vmem(1)[0],
        compiler_params=pltpu.CompilerParams(vmem_limit_bytes=16 << 20),
        cost_estimate=pl.CostEstimate(flops=order * order * 8, bytes_accessed=order * order * 12, transcendentals=0),
        name="unpack_stats",
    )(place, *stats)

    pieces = [total.astype(BF16)]
    for axis, shift, radix, splits in reversed(steps):
        if splits:
            whole = pieces[0] if len(pieces) == 1 else jnp.concatenate(pieces, axis=0)
            pieces = [whole] + [swap(whole, axis, digit << shift) for digit in range(1, radix)]

    result = jax.ShapeDtypeStruct((3, band, order), F32)
    square = (2, order, order)
    own, sent = pl.pallas_call(
        functools.partial(step_kernel, pieces=len(pieces), rows=rows, band=band),
        out_shape=(result, result),
        in_specs=[SMEM] + vmem(1 + len(pieces)),
        out_specs=tuple(vmem(2)),
        scratch_shapes=[
            pltpu.VMEM((order, order), BF16),
            pltpu.VMEM(square, F32),
            pltpu.VMEM(square, F32),
            pltpu.VMEM(square, F32),
            pltpu.VMEM(square, BF16),
            pltpu.VMEM(square, BF16),
            pltpu.VMEM(square, BF16),
            pltpu.VMEM((order, order), BF16),
            pltpu.VMEM((2 * band, order), BF16),
        ],
        compiler_params=pltpu.CompilerParams(vmem_limit_bytes=32 << 20),
        cost_estimate=pl.CostEstimate(flops=20 * order**3, bytes_accessed=order * order * 16, transcendentals=0),
        name="precondition",
    )(place, damped, *pieces)
    sent = swap(sent, "grp", 1)
    first = core == 0
    low, high = jnp.where(first, own, sent), jnp.where(first, sent, own)
    stats_new = stats_old + jnp.stack([low[0], high[0], low[1], high[1]])
    return stats_new, jnp.stack([low[2], high[2]])


def solution(mesh):
    in_specs = (P(("rep", "grp"), None), P(("rep", "grp"), None), P(None, "grp", None))
    out_specs = (P(None, "grp", None), P(None, "grp", None))
    return jax.shard_map(
        on_device, mesh=mesh, in_specs=in_specs, out_specs=out_specs, check_vma=False
    )
```

```python
import functools
import math

import jax
import jax.numpy as jnp
from jax import lax
from jax.experimental import pallas as pl
from jax.experimental.pallas import tpu as pltpu
from jax.sharding import PartitionSpec as P

F32 = jnp.float32
BF16 = jnp.bfloat16
DAMPING = 0.01
TILE = 16
LANES = 128
RADIX = 4


def swap(array, axis, mask):
    size = lax.axis_size(axis)
    return lax.ppermute(array, axis, [(i, i ^ mask) for i in range(size)])


def plan(axis, low, size, rows):
    steps = []
    shift, left = low + size.bit_length() - 1, size
    while left > 1:
        radix = min(RADIX, left)
        splits = rows // radix >= TILE and rows % radix == 0
        if not splits:
            radix = 2
        shift -= radix.bit_length() - 1
        left //= radix
        rows = rows // radix if splits else rows
        steps.append((axis, shift, radix, splits))
    return steps, rows


def vmem(count):
    return [pl.BlockSpec(memory_space=pltpu.VMEM)] * count


SMEM = pl.BlockSpec(memory_space=pltpu.SMEM)


def dot(a, b, contract=(1, 0)):
    return lax.dot_general(
        a, b, (((contract[0],), (contract[1],)), ((), ())), preferred_element_type=F32
    )


def term_kernel(place, grads, acts, out, *, other, rows):
    order = acts.shape[1]
    tile = place[0] ^ other
    columns = pl.ds(pl.multiple_of(tile * order, order), order)
    term = dot(grads[:, columns], acts[...], (0, 0))
    for block in range(order // rows):
        start = pl.multiple_of((block ^ place[1]) * rows, rows)
        out[pl.ds(start, rows), :] = term[block * rows : (block + 1) * rows]


def gradient_term(place, grads, acts, other, rows):
    tokens, order = acts.shape
    return pl.pallas_call(
        functools.partial(term_kernel, other=other, rows=rows),
        out_shape=jax.ShapeDtypeStruct((order, order), F32),
        in_specs=[SMEM] + vmem(2),
        out_specs=vmem(1)[0],
        compiler_params=pltpu.CompilerParams(vmem_limit_bytes=16 << 20),
        cost_estimate=pl.CostEstimate(
            flops=2 * tokens * order * order, bytes_accessed=4 * tokens * order, transcendentals=0
        ),
        name="gradient_term",
    )(place, grads, acts)


def on_diagonal(rows, columns, start):
    row = lax.broadcasted_iota(jnp.int32, (rows, columns), 0) + start
    return lax.broadcasted_iota(jnp.int32, (rows, columns), 1) == row


def halves_of(lines):
    others = lines - 1
    return {
        digit: [other for other in range(1, lines) if 0 < (other - digit) % others <= (others - 1) // 2]
        for digit in range(1, lines)
    }


def stage_kernel(place, stats, whole, *outs, tiles, lines):
    rows, order = stats.shape[1:]
    width = order // lines
    height = 2 * rows + TILE
    diagonal = on_diagonal(rows, order, place[3])
    row = lax.broadcasted_iota(jnp.int32, (TILE, order), 0)
    for other in range(2):
        tail = jnp.zeros((TILE, order), F32)
        for side in range(2):
            values = stats[side * tiles + (place[0] ^ other)]
            high = values.astype(BF16)
            low = other * height + side * rows
            whole[low : low + rows, :] = high
            rest = values - high.astype(F32)
            rest = jnp.sum(jnp.where(diagonal, rest, 0.0), axis=0, keepdims=True)
            middle = rest.astype(BF16).astype(F32)
            tail = jnp.where(row == 2 * side, middle, jnp.where(row == 2 * side + 1, rest - middle, tail))
        low = other * height + 2 * rows
        whole[low : low + TILE, :] = tail.astype(BF16)
    shares = halves_of(lines)
    for digit, out in enumerate(outs, 1):
        columns = [0] + [digit ^ other for other in shares[digit]]
        for index, column in enumerate(columns):
            start = pl.multiple_of((place[2] ^ column) * width, width)
            out[:, index * width : (index + 1) * width] = whole[:, pl.ds(start, width)]


def mirror_kernel(place, whole, swapped, *refs, rows):
    parts, out = refs[:-1], refs[-1]
    order = out.shape[2]
    lines = len(parts) + 1
    width = order // lines
    share = parts[0].shape[1] if parts else 0
    shares = halves_of(lines)
    diagonal = on_diagonal(width, width, 0)

    def at(digit):
        return pl.ds(pl.multiple_of((place[2] ^ digit) * width, width), width)

    def rows_of(digit, core):
        start = ((place[2] ^ digit) * 2 + (place[0] ^ core)) * rows
        return pl.ds(pl.multiple_of(start, rows), rows)

    def damp(side, digit, tails):
        vector = jnp.full((1, width), DAMPING, F32)
        for tail in tails:
            tail = tail.astype(F32)
            vector += tail[2 * side : 2 * side + 1] + tail[2 * side + 1 : 2 * side + 2]
        out[side, at(digit), at(digit)] += jnp.where(diagonal, vector, 0.0)

    for side in range(2):
        low, tail = slice(side * rows, (side + 1) * rows), slice(2 * rows, 2 * rows + TILE)
        out[side, rows_of(0, 0), :] = whole[low, :].astype(F32)
        out[side, rows_of(0, 1), :] = swapped[low, :order].astype(F32)
        for digit in range(1, lines):
            out[side, at(digit), at(0)] = out[side, at(0), at(digit)].T
        damp(side, 0, [whole[tail, at(0)], swapped[tail, at(0)]])
        for digit, part in enumerate(parts, 1):
            start = order + (digit - 1) * share
            for index, other in enumerate([digit] + shares[digit]):
                lanes = slice(index * width, (index + 1) * width)
                out[side, rows_of(digit, 0), at(other)] = part[low, lanes].astype(F32)
                lanes = slice(start + index * width, start + (index + 1) * width)
                out[side, rows_of(digit, 1), at(other)] = swapped[low, lanes].astype(F32)
                if index:
                    out[side, at(other), at(digit)] = out[side, at(digit), at(other)].T
            damp(side, digit, [part[tail, :width], swapped[tail, start : start + width]])


def collect_kernel(place, *refs, rows):
    parts, out = refs[:-1], refs[-1]
    order = out.shape[2]
    tail = slice(2 * rows, 2 * rows + TILE)
    vectors = [jnp.full((1, order), DAMPING, F32) for _ in range(2)]
    for part in parts:
        values = part[tail, :].astype(F32)
        for side in range(2):
            vectors[side] += values[2 * side : 2 * side + 1] + values[2 * side + 1 : 2 * side + 2]
    for index, part in enumerate(parts):
        start = ((place[2] ^ index // 2) * 2 + (place[0] ^ index % 2)) * rows
        start = pl.multiple_of(start, rows)
        diagonal = on_diagonal(rows, order, start)
        for side in range(2):
            values = part[side * rows : (side + 1) * rows, :].astype(F32)
            out[side, pl.ds(start, rows), :] = values + jnp.where(diagonal, vectors[side], 0.0)


def step_kernel(place, damped, *refs, pieces, rows, band):
    parts = refs[:pieces]
    own, sent, grad, gram, scaled, power, factors, offs, seconds, left_root, right_rows = refs[pieces:]
    order = grad.shape[0]
    for index, part in enumerate(parts):
        for low in range(0, part.shape[0], rows):
            block = (index * part.shape[0] + low) // rows
            start = pl.multiple_of((block ^ place[1]) * rows, rows)
            grad[pl.ds(start, rows), :] = part[low : low + rows, :]
    row_own = pl.ds(pl.multiple_of(place[3], band), band)
    row_sent = pl.ds(pl.multiple_of(place[4], band), band)
    step = min(order, 256)
    strips = [slice(low, low + step) for low in range(0, order, step)]
    eyes = [on_diagonal(step, order, low) for low in range(0, order, step)]
    sides = range(2)
    sums = [jnp.zeros((1, 1), F32) for _ in sides]
    for side in sides:
        gram[side] = dot(grad[...], grad[...], (side, side))
        for strip in strips:
            damp = gram[side, strip, :] + damped[side, strip, :]
            scaled[side, strip, :] = damp
            sums[side] += jnp.sum(damp * damp, keepdims=True)
        own[side] = gram[side, row_own, :]
        sent[side] = gram[side, row_sent, :]
    scales = [2.5 / jnp.sqrt(total) for total in sums]
    for side in sides:
        for strip, eye in zip(strips, eyes):
            iterate = scaled[side, strip, :] * scales[side]
            scaled[side, strip, :] = iterate
            factor = ((jnp.where(eye, 5.0, 0.0) - iterate) * 0.25).astype(BF16)
            factors[side, strip, :] = factor
            offs[side, strip, :] = (factor.astype(F32) - jnp.where(eye, 1.25, 0.0)).astype(BF16)
    across = [jnp.zeros((1, order), F32) for _ in sides]
    for side in sides:
        power[side] = dot(offs[side], offs[side])
        for strip, eye in zip(strips, eyes):
            value = power[side, strip, :] + 2.5 * offs[side, strip, :].astype(F32)
            power[side, strip, :] = value
            across[side] += jnp.sum(jnp.where(eye, value, 0.0), axis=0, keepdims=True)
            seconds[side, strip, :] = jnp.where(eye, 0.0, value).astype(BF16)
    beside = [jnp.zeros((1, order), F32) for _ in sides]
    for side in sides:
        gram[side] = dot(seconds[side], seconds[side])
        for strip, eye in zip(strips, eyes):
            value = power[side, strip, :]
            down = jnp.sum(jnp.where(eye, value, 0.0), axis=1, keepdims=True)
            value = gram[side, strip, :] + value * (3.125 + down + across[side]) - jnp.where(eye, down * down, 0.0)
            power[side, strip, :] = value
            beside[side] += jnp.sum(jnp.where(eye, value, 0.0), axis=0, keepdims=True)
            offs[side, strip, :] = jnp.where(eye, 0.0, value).astype(BF16)
            seconds[side, strip, :] = jnp.where(eye, 0.0, scaled[side, strip, :]).astype(BF16)
    for side in sides:
        gram[side] = dot(seconds[side], offs[side])
        for strip, eye in zip(strips, eyes):
            first, value = scaled[side, strip, :], power[side, strip, :]
            down = jnp.sum(jnp.where(eye, first, 0.0), axis=1, keepdims=True)
            iterate = gram[side, strip, :] + 2.44140625 * first + down * value
            iterate += jnp.where(eye, 0.0, first) * beside[side]
            factor = ((jnp.where(eye, 5.0, 0.0) - iterate) * 0.25).astype(BF16)
            offs[side, strip, :] = factor
    quarters = [jnp.sqrt(jnp.sqrt(scale)) for scale in scales]
    left_root[...] = (dot(factors[0], offs[0]) * quarters[0]).astype(BF16)
    right_rows[:band] = factors[1, row_own, :]
    right_rows[band:] = factors[1, row_sent, :]
    right_root = (dot(right_rows[...], offs[1]) * quarters[1]).astype(BF16)
    inner = dot(right_root, grad[...])
    high = inner.astype(BF16)
    low = (inner - high.astype(F32)).astype(BF16)
    update = (dot(high, left_root[...]) + dot(low, left_root[...])) * math.sqrt(order)
    own[2] = update[:band]
    sent[2] = update[band:]


def stage_stats(place, stats_old, tiles, lines):
    band, order = stats_old.shape[1:]
    height, width = 2 * (2 * band + TILE), order // lines
    mirrored = width % LANES == 0
    share = jax.ShapeDtypeStruct((height, width * (1 + (lines - 2) // 2)), BF16)
    outs = (jax.ShapeDtypeStruct((height, order), BF16),) + (share,) * (lines - 1 if mirrored else 0)
    whole, *shares = pl.pallas_call(
        functools.partial(stage_kernel, tiles=tiles, lines=lines),
        out_shape=outs,
        in_specs=[SMEM] + vmem(1),
        out_specs=tuple(vmem(len(outs))),
        compiler_params=pltpu.CompilerParams(vmem_limit_bytes=8 << 20),
        cost_estimate=pl.CostEstimate(flops=band * order * 20, bytes_accessed=band * order * 32, transcendentals=0),
        name="stage_stats",
    )(place, stats_old)
    return whole, shares if mirrored else [whole] * (lines - 1)


def whole_stats(place, whole, stats, order, band):
    height = 2 * band + TILE
    if stats and stats[0].shape[1] != order:
        swapped = swap(jnp.concatenate([part[height:] for part in (whole, *stats)], axis=1), "grp", 1)
        kernel, operands = mirror_kernel, [whole, swapped, *stats]
    else:
        swapped = swap(jnp.concatenate([part[height:] for part in (whole, *stats)], axis=0), "grp", 1)
        kernel, operands = collect_kernel, []
        for index, part in enumerate((whole, *stats)):
            operands += [part[:height], swapped[index * height : (index + 1) * height]]
    return pl.pallas_call(
        functools.partial(kernel, rows=band),
        out_shape=jax.ShapeDtypeStruct((2, order, order), F32),
        in_specs=[SMEM] + vmem(len(operands)),
        out_specs=vmem(1)[0],
        compiler_params=pltpu.CompilerParams(vmem_limit_bytes=16 << 20),
        cost_estimate=pl.CostEstimate(flops=order * order * 8, bytes_accessed=order * order * 12, transcendentals=0),
        name="whole_stats",
    )(place, *operands)


def on_device(activations, out_grads, stats_old):
    order = activations.shape[1]
    tiles = out_grads.shape[1] // order
    band = stats_old.shape[1]
    rep, grp = lax.axis_index("rep"), lax.axis_index("grp")
    reps, lines = lax.axis_size("rep"), lax.axis_size("grp") // 2
    core, line = grp & 1, grp >> 1

    across, rows = plan("rep", 0, reps, order)
    along, rows = plan("grp", 1, lines, rows)
    steps = across + along
    here = jnp.int32(0)
    for axis, shift, radix, halves in steps:
        if halves:
            here = here * radix + ((lax.axis_index(axis) >> shift) & (radix - 1))
    place = jnp.stack([core, here, line, grp * band, (grp ^ 1) * band]).astype(jnp.int32)

    sent = gradient_term(place, out_grads, activations, 1, rows)
    sent = swap(sent, "grp", 1)
    whole, shares = stage_stats(place, stats_old, tiles, lines)
    place, *shares = lax.optimization_barrier((place, *shares))
    stats = [swap(share, "grp", digit << 1) for digit, share in enumerate(shares, 1)]
    total = gradient_term(place, out_grads, activations, 0, rows)

    total = total + sent
    for index, (axis, shift, radix, splits) in enumerate(steps):
        if index == len(across):
            total, *stats = lax.optimization_barrier((total, *stats))
        if splits:
            total = total.reshape(radix, -1, order)
            parts = [swap(total[digit], axis, digit << shift) for digit in range(1, radix)]
            total = sum(parts, total[0])
        else:
            total = total + swap(total, axis, 1 << shift)
    damped = whole_stats(place, whole, stats, order, band)

    pieces = [total.astype(BF16)]
    for axis, shift, radix, splits in reversed(steps):
        if splits:
            whole = pieces[0] if len(pieces) == 1 else jnp.concatenate(pieces, axis=0)
            pieces = [whole] + [swap(whole, axis, digit << shift) for digit in range(1, radix)]

    result = jax.ShapeDtypeStruct((3, band, order), F32)
    square = (2, order, order)
    own, sent = pl.pallas_call(
        functools.partial(step_kernel, pieces=len(pieces), rows=rows, band=band),
        out_shape=(result, result),
        in_specs=[SMEM] + vmem(1 + len(pieces)),
        out_specs=tuple(vmem(2)),
        scratch_shapes=[
            pltpu.VMEM((order, order), BF16),
            pltpu.VMEM(square, F32),
            pltpu.VMEM(square, F32),
            pltpu.VMEM(square, F32),
            pltpu.VMEM(square, BF16),
            pltpu.VMEM(square, BF16),
            pltpu.VMEM(square, BF16),
            pltpu.VMEM((order, order), BF16),
            pltpu.VMEM((2 * band, order), BF16),
        ],
        compiler_params=pltpu.CompilerParams(vmem_limit_bytes=32 << 20),
        cost_estimate=pl.CostEstimate(flops=20 * order**3, bytes_accessed=order * order * 16, transcendentals=0),
        name="precondition",
    )(place, damped, *pieces)
    sent = swap(sent, "grp", 1)
    first = core == 0
    low, high = jnp.where(first, own, sent), jnp.where(first, sent, own)
    stats_new = stats_old + jnp.stack([low[0], high[0], low[1], high[1]])
    return stats_new, jnp.stack([low[2], high[2]])


def solution(mesh):
    in_specs = (P(("rep", "grp"), None), P(("rep", "grp"), None), P(None, "grp", None))
    out_specs = (P(None, "grp", None), P(None, "grp", None))
    return jax.shard_map(
        on_device, mesh=mesh, in_specs=in_specs, out_specs=out_specs, check_vma=False
    )
```

```python
import functools
import math

import jax
import jax.numpy as jnp
from jax import lax
from jax.experimental import pallas as pl
from jax.experimental.pallas import tpu as pltpu
from jax.sharding import PartitionSpec as P

F32 = jnp.float32
BF16 = jnp.bfloat16
DAMPING = 0.01
TILE = 16
LANES = 128


def swap(array, masks):
    reps, group = lax.axis_size("rep"), lax.axis_size("grp")
    pairs = []
    for rep in range(reps):
        for grp in range(group):
            over, along = masks[grp & 1]
            pairs.append((rep * group + grp, (rep ^ over) * group + (grp ^ along)))
    return lax.ppermute(array, ("rep", "grp"), pairs)


CORES = ((0, 1), (0, 1))


def both(first, second):
    return tuple((a[0] ^ b[0], a[1] ^ b[1]) for a, b in zip(first, second))


def plan(reps, lines, rows):
    over = [(1 << bit, 0) for bit in range(reps.bit_length() - 1)]
    along = [(0, 2 << bit) for bit in range(lines.bit_length() - 1)]
    phases = []
    for kind, bits in (("relay", list(zip(over, over[::-1]))), ("direct", list(zip(along, along)))):
        while bits:
            if len(bits) > 1 and rows // 4 >= TILE:
                phases.append((kind, bits[:2]))
                bits, rows = bits[2:], rows // 4
            elif rows // 2 >= TILE:
                phases.append(("halve", bits[:1]))
                bits, rows = bits[1:], rows // 2
            else:
                phases.append(("add", bits[:1]))
                bits = bits[1:]
    return phases, rows


def position(phases, core, rep, grp):
    here = jnp.int32(0)
    for kind, bits in phases:
        if kind != "add":
            for masks in bits:
                flags = [jnp.where((rep & over) | (grp & along), 1, 0) for over, along in masks]
                here = here * 2 + jnp.where(core == 0, flags[0], flags[1])
    return here


def reduce_phase(total, kind, bits, early=()):
    if kind == "add":
        return total + swap(total, bits[0])
    if kind == "halve":
        keep, send = jnp.split(total, 2)
        return keep + swap(send, bits[0])
    keep, second, first, last = jnp.split(total, 4)
    if kind == "relay":
        last = swap(last, bits[0])
        first = swap(first, bits[0])
        last = lax.optimization_barrier((last, *early))[0]
        second = swap(second + last, bits[1])
        return keep + first + second
    second, first, last = swap(second, bits[1]), swap(first, bits[0]), swap(last, both(*bits))
    return keep + second + first + last


def gather_phase(whole, kind, bits):
    if kind == "add":
        return [whole]
    if kind == "halve":
        return [whole, swap(whole, bits[0])]
    return [whole, swap(whole, bits[1]), swap(whole, bits[0]), swap(whole, both(*bits))]


def vmem(count):
    return [pl.BlockSpec(memory_space=pltpu.VMEM)] * count


SMEM = pl.BlockSpec(memory_space=pltpu.SMEM)


def dot(a, b, contract=(1, 0)):
    return lax.dot_general(
        a, b, (((contract[0],), (contract[1],)), ((), ())), preferred_element_type=F32
    )


def term_kernel(place, grads, acts, out, *, other, rows):
    order = acts.shape[1]
    columns = pl.ds(pl.multiple_of((place[0] ^ other) * order, order), order)
    term = dot(grads[:, columns], acts[...], (0, 0))
    for block in range(order // rows):
        there = pl.ds(pl.multiple_of((block ^ place[6 if other else 1]) * rows, rows), rows)
        out[there, :] = term[block * rows : (block + 1) * rows]


def gradient_term(place, grads, acts, other, rows):
    tokens, order = acts.shape
    return pl.pallas_call(
        functools.partial(term_kernel, other=other, rows=rows),
        out_shape=jax.ShapeDtypeStruct((order, order), F32),
        in_specs=[SMEM] + vmem(2),
        out_specs=vmem(1)[0],
        compiler_params=pltpu.CompilerParams(vmem_limit_bytes=16 << 20),
        cost_estimate=pl.CostEstimate(
            flops=2 * tokens * order * order, bytes_accessed=4 * tokens * order, transcendentals=0
        ),
        name="gradient_term",
    )(place, grads, acts)


def on_diagonal(rows, columns, start):
    row = lax.broadcasted_iota(jnp.int32, (rows, columns), 0) + start
    return lax.broadcasted_iota(jnp.int32, (rows, columns), 1) == row


def columns_for(digit, lines):
    return [0] + [digit ^ other for other in range(digit + 1, lines)]


def stage_kernel(place, stats, whole, *outs, tiles, lines):
    rows, order = stats.shape[1:]
    width = order // lines
    height = rows + TILE
    diagonal = on_diagonal(rows, order, place[3])
    row = lax.broadcasted_iota(jnp.int32, (TILE, order), 0)
    for other in range(2):
        for side in range(2):
            values = stats[(place[5] ^ side) * tiles + (place[0] ^ other)]
            high = values.astype(BF16)
            low = (2 * other + side) * height
            whole[low : low + rows, :] = high
            rest = values - high.astype(F32)
            rest = jnp.sum(jnp.where(diagonal, rest, 0.0), axis=0, keepdims=True)
            middle = rest.astype(BF16).astype(F32)
            tail = jnp.where(row == 0, middle, jnp.where(row == 1, rest - middle, 0.0))
            whole[low + rows : low + height, :] = tail.astype(BF16)
    for digit, out in enumerate(outs, 1):
        for index, column in enumerate(columns_for(digit, lines)):
            start = pl.multiple_of((place[2] ^ column) * width, width)
            for other in range(2):
                low = 2 * other * height
                values = whole[low : low + height, pl.ds(start, width)]
                out[other * height : (other + 1) * height, index * width : (index + 1) * width] = values


def mirror_kernel(place, whole, swapped, mine, turned, out, *, rows, lines):
    order = out.shape[2]
    width = order // lines
    height = rows + TILE
    diagonal = on_diagonal(width, width, 0)

    def at(digit):
        return pl.ds(pl.multiple_of((place[2] ^ digit) * width, width), width)

    def rows_of(digit, core):
        start = ((place[2] ^ digit) * 2 + (place[0] ^ core)) * rows
        return pl.ds(pl.multiple_of(start, rows), rows)

    for index, part in enumerate((mine, turned)):
        side = place[5] ^ index
        low = slice(index * height, index * height + rows)
        tail = slice(index * height + rows, (index + 1) * height)

        def damp(digit, tails):
            tails = [values.astype(F32) for values in tails]
            vector = sum((values[:1] + values[1:2] for values in tails), jnp.full((1, width), DAMPING, F32))
            out[side, at(digit), at(digit)] += jnp.where(diagonal, vector, 0.0)

        out[side, rows_of(0, 0), :] = whole[low, :].astype(F32)
        out[side, rows_of(0, 1), :] = swapped[low, :order].astype(F32)
        for digit in range(1, lines):
            out[side, at(digit), at(0)] = out[side, at(0), at(digit)].T
        damp(0, [whole[tail, at(0)], swapped[tail, at(0)]])
        start = 0
        for digit in range(1, lines):
            first = slice(start, start + width)
            for column in columns_for(digit, lines):
                other = digit ^ column
                lanes = slice(start, start + width)
                out[side, rows_of(digit, 0), at(other)] = part[:rows, lanes].astype(F32)
                lanes = slice(order + start, order + start + width)
                out[side, rows_of(digit, 1), at(other)] = swapped[low, lanes].astype(F32)
                if column:
                    out[side, at(other), at(digit)] = out[side, at(digit), at(other)].T
                start += width
            away = slice(order + first.start, order + first.stop)
            damp(digit, [part[rows:height, first], swapped[tail, away]])


def collect_kernel(place, *refs, rows):
    parts, out = refs[:-1], refs[-1]
    order = out.shape[2]
    height = rows + TILE
    for index in range(2):
        side = place[5] ^ index
        vector = jnp.full((1, order), DAMPING, F32)
        for part in parts:
            tail = part[index * height + rows : (index + 1) * height, :].astype(F32)
            vector += tail[:1] + tail[1:2]
        for number, part in enumerate(parts):
            start = ((place[2] ^ number // 2) * 2 + (place[0] ^ number % 2)) * rows
            start = pl.multiple_of(start, rows)
            values = part[index * height : index * height + rows, :].astype(F32)
            out[side, pl.ds(start, rows), :] = values + jnp.where(on_diagonal(rows, order, start), vector, 0.0)


def step_kernel(place, damped, *refs, pieces, rows, band):
    parts = refs[:pieces]
    own, sent, grad, gram, scaled, power, factors, offs, seconds, left_root, right_rows = refs[pieces:]
    order = grad.shape[0]
    for index, part in enumerate(parts):
        for low in range(0, part.shape[0], rows):
            block = (index * part.shape[0] + low) // rows
            start = pl.multiple_of((block ^ place[1]) * rows, rows)
            grad[pl.ds(start, rows), :] = part[low : low + rows, :]
    for side in range(2):
        gram[side] = dot(grad[...], grad[...], (side, side))
        own[side] = gram[side, pl.ds(pl.multiple_of(place[3], band), band), :]
        sent[side] = gram[side, pl.ds(pl.multiple_of(place[4], band), band), :]
    step = min(order, LANES)
    strips = [slice(low, low + step) for low in range(0, order, step)]
    eye = on_diagonal(step, step, 0)
    sides = range(2)

    def on_eye(block):
        return jnp.where(eye, block, 0.0)

    def beside(block):
        return jnp.sum(on_eye(block), axis=1, keepdims=True)

    def above(ref, side):
        blocks = [jnp.sum(on_eye(ref[side, strip, strip]), axis=0, keepdims=True) for strip in strips]
        return jnp.concatenate(blocks, axis=1)

    def off_eye(ref, side, strip, values):
        ref[side, strip, :] = values.astype(BF16)
        ref[side, strip, strip] = jnp.where(eye, 0.0, values[:, strip]).astype(BF16)

    scales = []
    for side in sides:
        total = jnp.zeros((8, order), F32)
        for strip in strips:
            value = gram[side, strip, :] + damped[side, strip, :]
            scaled[side, strip, :] = value
            total += jnp.sum((value * value).reshape(step // 8, 8, order), axis=0)
        scales.append(2.5 / jnp.sqrt(jnp.sum(total, keepdims=True)))

    def iterate(side, strip):
        return scaled[side, strip, :] * scales[side]

    for side in sides:
        for strip in strips:
            value = iterate(side, strip)
            factors[side, strip, :] = (value * -0.25).astype(BF16)
            block = (jnp.where(eye, 5.0, 0.0) - value[:, strip]) * 0.25
            factors[side, strip, strip] = block.astype(BF16)
    for side in sides:
        square = dot(factors[side], factors[side])
        for strip in strips:
            value = square[strip]
            power[side, strip, :] = value
            power[side, strip, strip] = value[:, strip] - jnp.where(eye, 1.5625, 0.0)
            off_eye(seconds, side, strip, value)
    for side in sides:
        square = dot(seconds[side], seconds[side])
        across = above(power, side) + 3.125
        for strip in strips:
            value = power[side, strip, :]
            down = beside(value[:, strip])
            value = square[strip] + value * (across + down)
            power[side, strip, :] = value
            power[side, strip, strip] = value[:, strip] - on_eye(down * down)
            off_eye(offs, side, strip, value)
            off_eye(seconds, side, strip, iterate(side, strip))
    for side in sides:
        product = dot(seconds[side], offs[side])
        across = above(power, side)
        for strip in strips:
            first, value = iterate(side, strip), power[side, strip, :]
            down = beside(first[:, strip])
            value = product[strip] + first * (across + 2.44140625) + down * value
            offs[side, strip, :] = (value * -0.25).astype(BF16)
            block = jnp.where(eye, 5.0 + down * across[:, strip], 0.0) - value[:, strip]
            offs[side, strip, strip] = (block * 0.25).astype(BF16)
    quarters = [jnp.sqrt(jnp.sqrt(scale)) for scale in scales]
    left_root[...] = (dot(factors[0], offs[0]) * quarters[0]).astype(BF16)
    right_rows[:band] = factors[1, pl.ds(pl.multiple_of(place[3], band), band), :]
    right_rows[band:] = factors[1, pl.ds(pl.multiple_of(place[4], band), band), :]
    right_root = (dot(right_rows[...], offs[1]) * quarters[1]).astype(BF16)
    inner = dot(right_root, grad[...])
    high = inner.astype(BF16)
    low = (inner - high.astype(F32)).astype(BF16)
    update = (dot(high, left_root[...]) + dot(low, left_root[...])) * math.sqrt(order)
    own[2] = update[:band]
    sent[2] = update[band:]


def stage_stats(place, stats_old, tiles, lines):
    band, order = stats_old.shape[1:]
    height, width = band + TILE, order // lines
    outs = [jax.ShapeDtypeStruct((4 * height, order), BF16)]
    for number in range(1, lines if width % LANES == 0 else 1):
        outs.append(jax.ShapeDtypeStruct((2 * height, width * len(columns_for(number, lines))), BF16))
    return pl.pallas_call(
        functools.partial(stage_kernel, tiles=tiles, lines=lines),
        out_shape=tuple(outs),
        in_specs=[SMEM] + vmem(1),
        out_specs=tuple(vmem(len(outs))),
        compiler_params=pltpu.CompilerParams(vmem_limit_bytes=8 << 20),
        cost_estimate=pl.CostEstimate(flops=band * order * 20, bytes_accessed=band * order * 32, transcendentals=0),
        name="stage_stats",
    )(place, stats_old)


def whole_stats(place, whole, stats, lines, order, band):
    height = band + TILE
    if order // lines % LANES == 0:
        mine = jnp.concatenate(stats, axis=1)
        turned = swap(mine, ((1, 0), (1, 0)))
        away = jnp.concatenate([mine[height:], turned[height:]], axis=0)
        swapped = swap(jnp.concatenate([whole[2 * height :], away], axis=1), CORES)
        kernel = functools.partial(mirror_kernel, rows=band, lines=lines)
        operands = [whole, swapped, mine, turned]
    else:
        swapped = swap(jnp.concatenate([part[2 * height :] for part in (whole, *stats)], axis=0), CORES)
        kernel, operands = functools.partial(collect_kernel, rows=band), []
        for index, part in enumerate((whole, *stats)):
            operands += [part[: 2 * height], swapped[index * 2 * height : (index + 1) * 2 * height]]
    return pl.pallas_call(
        kernel,
        out_shape=jax.ShapeDtypeStruct((2, order, order), F32),
        in_specs=[SMEM] + vmem(len(operands)),
        out_specs=vmem(1)[0],
        compiler_params=pltpu.CompilerParams(vmem_limit_bytes=16 << 20),
        cost_estimate=pl.CostEstimate(flops=order * order * 8, bytes_accessed=order * order * 12, transcendentals=0),
        name="whole_stats",
    )(place, *operands)


def on_device(activations, out_grads, stats_old):
    order = activations.shape[1]
    tiles = out_grads.shape[1] // order
    band = stats_old.shape[1]
    rep, grp = lax.axis_index("rep"), lax.axis_index("grp")
    reps, lines = lax.axis_size("rep"), lax.axis_size("grp") // 2
    core, line = grp & 1, grp >> 1

    phases, rows = plan(reps, lines, order)
    here, beside = (position(phases, core ^ other, rep, grp) for other in (0, 1))
    place = jnp.stack([core, here, line, grp * band, (grp ^ 1) * band, rep & 1, beside]).astype(jnp.int32)

    sent = swap(gradient_term(place, out_grads, activations, 1, rows), CORES)
    whole, *shares = stage_stats(place, stats_old, tiles, lines)
    place, *shares = lax.optimization_barrier((place, *shares))
    stats = [swap(share, ((0, 2 * step),) * 2) for step, share in enumerate(shares or [whole] * (lines - 1), 1)]
    total = gradient_term(place, out_grads, activations, 0, rows) + sent
    for index, (kind, bits) in enumerate(phases):
        if index == (reps > 1):
            total, *stats = lax.optimization_barrier((total, *stats))
        total = reduce_phase(total, kind, bits, [] if index else [stats[-1]])
    damped = whole_stats(place, whole, stats, lines, order, band)

    pieces = [total.astype(BF16)]
    for kind, bits in reversed(phases):
        joined = pieces[0] if len(pieces) == 1 else jnp.concatenate(pieces, axis=0)
        pieces = gather_phase(joined, kind, bits)

    result = jax.ShapeDtypeStruct((3, band, order), F32)
    square = (2, order, order)
    own, sent = pl.pallas_call(
        functools.partial(step_kernel, pieces=len(pieces), rows=rows, band=band),
        out_shape=(result, result),
        in_specs=[SMEM] + vmem(1 + len(pieces)),
        out_specs=tuple(vmem(2)),
        scratch_shapes=[
            pltpu.VMEM((order, order), BF16),
            pltpu.VMEM(square, F32),
            pltpu.VMEM(square, F32),
            pltpu.VMEM(square, F32),
            pltpu.VMEM(square, BF16),
            pltpu.VMEM(square, BF16),
            pltpu.VMEM(square, BF16),
            pltpu.VMEM((order, order), BF16),
            pltpu.VMEM((2 * band, order), BF16),
        ],
        compiler_params=pltpu.CompilerParams(vmem_limit_bytes=32 << 20),
        cost_estimate=pl.CostEstimate(flops=20 * order**3, bytes_accessed=order * order * 16, transcendentals=0),
        name="precondition",
    )(place, damped, *pieces)
    sent = swap(sent, CORES)
    own_tile = lax.broadcasted_iota(jnp.int32, (1, tiles, 1, 1), 1) == core
    moved = jnp.where(own_tile, own[:2, None], sent[:2, None]).reshape(stats_old.shape)
    return stats_old + moved, jnp.where(own_tile[0], own[2][None], sent[2][None])


def solution(mesh):
    in_specs = (P(("rep", "grp"), None), P(("rep", "grp"), None), P(None, "grp", None))
    out_specs = (P(None, "grp", None), P(None, "grp", None))
    return jax.shard_map(
        on_device, mesh=mesh, in_specs=in_specs, out_specs=out_specs, check_vma=False
    )
```

```python
import functools
import math

import jax
import jax.numpy as jnp
from jax import lax
from jax.experimental import pallas as pl
from jax.experimental.pallas import tpu as pltpu
from jax.sharding import PartitionSpec as P

F32 = jnp.float32
BF16 = jnp.bfloat16
DAMPING = 0.01
TILE = 16
LANES = 128


def swap(array, masks):
    reps, group = lax.axis_size("rep"), lax.axis_size("grp")
    pairs = []
    for rep in range(reps):
        for grp in range(group):
            over, along = masks[grp & 1]
            pairs.append((rep * group + grp, (rep ^ over) * group + (grp ^ along)))
    return lax.ppermute(array, ("rep", "grp"), pairs)


CORES = ((0, 1), (0, 1))


def both(first, second):
    return tuple((a[0] ^ b[0], a[1] ^ b[1]) for a, b in zip(first, second))


def plan(reps, lines, rows):
    over = [(1 << bit, 0) for bit in range(reps.bit_length() - 1)]
    along = [(0, 2 << bit) for bit in range(lines.bit_length() - 1)]
    phases = []
    for kind, bits in (("relay", list(zip(over, over[::-1]))), ("direct", list(zip(along, along)))):
        while bits:
            if len(bits) > 1 and rows // 4 >= TILE:
                phases.append((kind, bits[:2]))
                bits, rows = bits[2:], rows // 4
            elif rows // 2 >= TILE:
                phases.append(("halve", bits[:1]))
                bits, rows = bits[1:], rows // 2
            else:
                phases.append(("add", bits[:1]))
                bits = bits[1:]
    return phases, rows


def position(phases, core, rep, grp):
    here = jnp.int32(0)
    for kind, bits in phases:
        if kind != "add":
            for masks in bits:
                flags = [jnp.where((rep & over) | (grp & along), 1, 0) for over, along in masks]
                here = here * 2 + jnp.where(core == 0, flags[0], flags[1])
    return here


def reduce_phase(total, kind, bits, early=()):
    if kind == "add":
        return total + swap(total, bits[0])
    if kind == "halve":
        keep, send = jnp.split(total, 2)
        return keep + swap(send, bits[0])
    keep, second, first, last = jnp.split(total, 4)
    if kind == "relay":
        last = swap(last, bits[0])
        first = swap(first, bits[0])
        last = lax.optimization_barrier((last, *early))[0]
        second = swap(second + last, bits[1])
        return keep + first + second
    second, first, last = swap(second, bits[1]), swap(first, bits[0]), swap(last, both(*bits))
    return keep + second + first + last


def gather_phase(whole, kind, bits):
    if kind == "add":
        return [whole]
    if kind == "halve":
        return [whole, swap(whole, bits[0])]
    return [whole, swap(whole, bits[1]), swap(whole, bits[0]), swap(whole, both(*bits))]


def vmem(count):
    return [pl.BlockSpec(memory_space=pltpu.VMEM)] * count


SMEM = pl.BlockSpec(memory_space=pltpu.SMEM)


def dot(a, b, contract=(1, 0)):
    return lax.dot_general(
        a, b, (((contract[0],), (contract[1],)), ((), ())), preferred_element_type=F32
    )


def term_kernel(place, grads, acts, out, *, other, rows):
    order = acts.shape[1]
    columns = pl.ds(pl.multiple_of((place[0] ^ other) * order, order), order)
    term = dot(grads[:, columns], acts[...], (0, 0))
    for block in range(order // rows):
        there = pl.ds(pl.multiple_of((block ^ place[6 if other else 1]) * rows, rows), rows)
        out[there, :] = term[block * rows : (block + 1) * rows]


def gradient_term(place, grads, acts, other, rows):
    tokens, order = acts.shape
    return pl.pallas_call(
        functools.partial(term_kernel, other=other, rows=rows),
        out_shape=jax.ShapeDtypeStruct((order, order), F32),
        in_specs=[SMEM] + vmem(2),
        out_specs=vmem(1)[0],
        compiler_params=pltpu.CompilerParams(vmem_limit_bytes=16 << 20),
        cost_estimate=pl.CostEstimate(
            flops=2 * tokens * order * order, bytes_accessed=4 * tokens * order, transcendentals=0
        ),
        name="gradient_term",
    )(place, grads, acts)


def on_diagonal(rows, columns, start):
    row = lax.broadcasted_iota(jnp.int32, (rows, columns), 0) + start
    return lax.broadcasted_iota(jnp.int32, (rows, columns), 1) == row


def columns_for(digit, lines):
    return [0] + [digit ^ other for other in range(digit + 1, lines)]


def stage_kernel(place, stats, whole, *outs, tiles, lines):
    rows, order = stats.shape[1:]
    width = order // lines
    height = rows + TILE
    diagonal = on_diagonal(rows, order, place[3])
    row = lax.broadcasted_iota(jnp.int32, (TILE, order), 0)
    for other in range(2):
        for side in range(2):
            values = stats[(place[5] ^ side) * tiles + (place[0] ^ other)]
            high = values.astype(BF16)
            low = (2 * other + side) * height
            whole[low : low + rows, :] = high
            rest = values - high.astype(F32)
            rest = jnp.sum(jnp.where(diagonal, rest, 0.0), axis=0, keepdims=True)
            middle = rest.astype(BF16).astype(F32)
            tail = jnp.where(row == 0, middle, jnp.where(row == 1, rest - middle, 0.0))
            whole[low + rows : low + height, :] = tail.astype(BF16)
    for digit, out in enumerate(outs, 1):
        for index, column in enumerate(columns_for(digit, lines)):
            start = pl.multiple_of((place[2] ^ column) * width, width)
            for other in range(2):
                low = 2 * other * height
                values = whole[low : low + height, pl.ds(start, width)]
                out[other * height : (other + 1) * height, index * width : (index + 1) * width] = values


def mirror_kernel(place, whole, swapped, mine, turned, out, *, rows, lines):
    order = out.shape[2]
    width = order // lines
    height = rows + TILE
    diagonal = on_diagonal(width, width, 0)

    def at(digit):
        return pl.ds(pl.multiple_of((place[2] ^ digit) * width, width), width)

    def rows_of(digit, core):
        start = ((place[2] ^ digit) * 2 + (place[0] ^ core)) * rows
        return pl.ds(pl.multiple_of(start, rows), rows)

    for index, part in enumerate((mine, turned)):
        side = place[5] ^ index
        low = slice(index * height, index * height + rows)
        tail = slice(index * height + rows, (index + 1) * height)

        def damp(digit, tails):
            tails = [values.astype(F32) for values in tails]
            vector = sum((values[:1] + values[1:2] for values in tails), jnp.full((1, width), DAMPING, F32))
            out[side, at(digit), at(digit)] += jnp.where(diagonal, vector, 0.0)

        out[side, rows_of(0, 0), :] = whole[low, :].astype(F32)
        out[side, rows_of(0, 1), :] = swapped[low, :order].astype(F32)
        for digit in range(1, lines):
            out[side, at(digit), at(0)] = out[side, at(0), at(digit)].T
        damp(0, [whole[tail, at(0)], swapped[tail, at(0)]])
        start = 0
        for digit in range(1, lines):
            first = slice(start, start + width)
            for column in columns_for(digit, lines):
                other = digit ^ column
                lanes = slice(start, start + width)
                out[side, rows_of(digit, 0), at(other)] = part[:rows, lanes].astype(F32)
                lanes = slice(order + start, order + start + width)
                out[side, rows_of(digit, 1), at(other)] = swapped[low, lanes].astype(F32)
                if column:
                    out[side, at(other), at(digit)] = out[side, at(digit), at(other)].T
                start += width
            away = slice(order + first.start, order + first.stop)
            damp(digit, [part[rows:height, first], swapped[tail, away]])


def collect_kernel(place, *refs, rows):
    parts, out = refs[:-1], refs[-1]
    order = out.shape[2]
    height = rows + TILE
    for index in range(2):
        side = place[5] ^ index
        vector = jnp.full((1, order), DAMPING, F32)
        for part in parts:
            tail = part[index * height + rows : (index + 1) * height, :].astype(F32)
            vector += tail[:1] + tail[1:2]
        for number, part in enumerate(parts):
            start = ((place[2] ^ number // 2) * 2 + (place[0] ^ number % 2)) * rows
            start = pl.multiple_of(start, rows)
            values = part[index * height : index * height + rows, :].astype(F32)
            out[side, pl.ds(start, rows), :] = values + jnp.where(on_diagonal(rows, order, start), vector, 0.0)


def step_kernel(place, damped, stats, *refs, pieces, rows, band):
    parts = refs[:pieces]
    fresh, own, sent, grad, gram, scaled, power, factors, offs, seconds, left_root, right_rows, added, sems = refs[pieces:]
    tiles = stats.shape[0] // 2
    order = grad.shape[0]
    for index, part in enumerate(parts):
        for low in range(0, part.shape[0], rows):
            block = (index * part.shape[0] + low) // rows
            start = pl.multiple_of((block ^ place[1]) * rows, rows)
            grad[pl.ds(start, rows), :] = part[low : low + rows, :]
    copies = []
    for side in range(2):
        gram[side] = dot(grad[...], grad[...], (side, side))
        chain = side * tiles + place[0]
        added[side] = stats[chain] + gram[side, pl.ds(pl.multiple_of(place[3], band), band), :]
        copies.append(pltpu.make_async_copy(added.at[side], fresh.at[chain], sems.at[side]))
        copies[side].start()
        sent[side] = gram[side, pl.ds(pl.multiple_of(place[4], band), band), :]
    step = min(order, LANES)
    strips = [slice(low, low + step) for low in range(0, order, step)]
    eye = on_diagonal(step, step, 0)
    sides = range(2)

    def on_eye(block):
        return jnp.where(eye, block, 0.0)

    def beside(block):
        return jnp.sum(on_eye(block), axis=1, keepdims=True)

    def above(ref, side):
        blocks = [jnp.sum(on_eye(ref[side, strip, strip]), axis=0, keepdims=True) for strip in strips]
        return jnp.concatenate(blocks, axis=1)

    def off_eye(ref, side, strip, values):
        ref[side, strip, :] = values.astype(BF16)
        ref[side, strip, strip] = jnp.where(eye, 0.0, values[:, strip]).astype(BF16)

    scales = []
    for side in sides:
        total = jnp.zeros((8, order), F32)
        for strip in strips:
            value = gram[side, strip, :] + damped[side, strip, :]
            scaled[side, strip, :] = value
            total += jnp.sum((value * value).reshape(step // 8, 8, order), axis=0)
        scales.append(2.5 / jnp.sqrt(jnp.sum(total, keepdims=True)))

    def iterate(side, strip):
        return scaled[side, strip, :] * scales[side]

    for side in sides:
        for strip in strips:
            value = iterate(side, strip)
            factors[side, strip, :] = (value * -0.25).astype(BF16)
            block = (jnp.where(eye, 5.0, 0.0) - value[:, strip]) * 0.25
            factors[side, strip, strip] = block.astype(BF16)
    for side in sides:
        square = dot(factors[side], factors[side])
        for strip in strips:
            value = square[strip]
            power[side, strip, :] = value
            power[side, strip, strip] = value[:, strip] - jnp.where(eye, 1.5625, 0.0)
            off_eye(seconds, side, strip, value)
    for side in sides:
        square = dot(seconds[side], seconds[side])
        across = above(power, side) + 3.125
        for strip in strips:
            value = power[side, strip, :]
            down = beside(value[:, strip])
            value = square[strip] + value * (across + down)
            power[side, strip, :] = value
            power[side, strip, strip] = value[:, strip] - on_eye(down * down)
            off_eye(offs, side, strip, value)
            off_eye(seconds, side, strip, iterate(side, strip))
    for side in sides:
        product = dot(seconds[side], offs[side])
        across = above(power, side)
        for strip in strips:
            first, value = iterate(side, strip), power[side, strip, :]
            down = beside(first[:, strip])
            value = product[strip] + first * (across + 2.44140625) + down * value
            offs[side, strip, :] = (value * -0.25).astype(BF16)
            block = jnp.where(eye, 5.0 + down * across[:, strip], 0.0) - value[:, strip]
            offs[side, strip, strip] = (block * 0.25).astype(BF16)
    quarters = [jnp.sqrt(jnp.sqrt(scale)) for scale in scales]
    left_root[...] = (dot(factors[0], offs[0]) * quarters[0]).astype(BF16)
    right_rows[:band] = factors[1, pl.ds(pl.multiple_of(place[3], band), band), :]
    right_rows[band:] = factors[1, pl.ds(pl.multiple_of(place[4], band), band), :]
    right_root = (dot(right_rows[...], offs[1]) * quarters[1]).astype(BF16)
    inner = dot(right_root, grad[...])
    high = inner.astype(BF16)
    low = (inner - high.astype(F32)).astype(BF16)
    update = (dot(high, left_root[...]) + dot(low, left_root[...])) * math.sqrt(order)
    own[...] = update[:band]
    sent[2] = update[band:]
    for copy in copies:
        copy.wait()


def finish_kernel(place, fresh, stats, own, sent, out, update, added, sems):
    tiles = update.shape[0]
    other = 1 - place[0]
    copies = [
        pltpu.make_async_copy(own, update.at[place[0]], sems.at[0]),
        pltpu.make_async_copy(sent.at[2], update.at[other], sems.at[1]),
    ]
    for side in range(2):
        chain = side * tiles + other
        added[side] = stats[chain] + sent[side]
        copies.append(pltpu.make_async_copy(added.at[side], out.at[chain], sems.at[2 + side]))
    for copy in copies:
        copy.start()
    for copy in copies:
        copy.wait()


def stage_stats(place, stats_old, tiles, lines):
    band, order = stats_old.shape[1:]
    height, width = band + TILE, order // lines
    outs = [jax.ShapeDtypeStruct((4 * height, order), BF16)]
    for number in range(1, lines if width % LANES == 0 else 1):
        outs.append(jax.ShapeDtypeStruct((2 * height, width * len(columns_for(number, lines))), BF16))
    return pl.pallas_call(
        functools.partial(stage_kernel, tiles=tiles, lines=lines),
        out_shape=tuple(outs),
        in_specs=[SMEM] + vmem(1),
        out_specs=tuple(vmem(len(outs))),
        compiler_params=pltpu.CompilerParams(vmem_limit_bytes=8 << 20),
        cost_estimate=pl.CostEstimate(flops=band * order * 20, bytes_accessed=band * order * 32, transcendentals=0),
        name="stage_stats",
    )(place, stats_old)


def whole_stats(place, whole, stats, lines, order, band):
    height = band + TILE
    if order // lines % LANES == 0:
        mine = jnp.concatenate(stats, axis=1)
        turned = swap(mine, ((1, 0), (1, 0)))
        away = jnp.concatenate([mine[height:], turned[height:]], axis=0)
        swapped = swap(jnp.concatenate([whole[2 * height :], away], axis=1), CORES)
        kernel = functools.partial(mirror_kernel, rows=band, lines=lines)
        operands = [whole, swapped, mine, turned]
    else:
        swapped = swap(jnp.concatenate([part[2 * height :] for part in (whole, *stats)], axis=0), CORES)
        kernel, operands = functools.partial(collect_kernel, rows=band), []
        for index, part in enumerate((whole, *stats)):
            operands += [part[: 2 * height], swapped[index * 2 * height : (index + 1) * 2 * height]]
    return pl.pallas_call(
        kernel,
        out_shape=jax.ShapeDtypeStruct((2, order, order), F32),
        in_specs=[SMEM] + vmem(len(operands)),
        out_specs=vmem(1)[0],
        compiler_params=pltpu.CompilerParams(vmem_limit_bytes=16 << 20),
        cost_estimate=pl.CostEstimate(flops=order * order * 8, bytes_accessed=order * order * 12, transcendentals=0),
        name="whole_stats",
    )(place, *operands)


def on_device(activations, out_grads, stats_old):
    order = activations.shape[1]
    tiles = out_grads.shape[1] // order
    band = stats_old.shape[1]
    rep, grp = lax.axis_index("rep"), lax.axis_index("grp")
    reps, lines = lax.axis_size("rep"), lax.axis_size("grp") // 2
    core, line = grp & 1, grp >> 1

    phases, rows = plan(reps, lines, order)
    here, beside = (position(phases, core ^ other, rep, grp) for other in (0, 1))
    place = jnp.stack([core, here, line, grp * band, (grp ^ 1) * band, rep & 1, beside]).astype(jnp.int32)

    sent = swap(gradient_term(place, out_grads, activations, 1, rows), CORES)
    whole, *shares = stage_stats(place, stats_old, tiles, lines)
    place, *shares = lax.optimization_barrier((place, *shares))
    stats = [swap(share, ((0, 2 * step),) * 2) for step, share in enumerate(shares or [whole] * (lines - 1), 1)]
    total = gradient_term(place, out_grads, activations, 0, rows) + sent
    for index, (kind, bits) in enumerate(phases):
        if index == (reps > 1):
            total, *stats = lax.optimization_barrier((total, *stats))
        total = reduce_phase(total, kind, bits, [] if index else [stats[-1]])
    damped = whole_stats(place, whole, stats, lines, order, band)

    pieces = [total.astype(BF16)]
    for kind, bits in reversed(phases):
        joined = pieces[0] if len(pieces) == 1 else jnp.concatenate(pieces, axis=0)
        pieces = gather_phase(joined, kind, bits)

    rows_pair = (2, band, order)
    square = (2, order, order)
    anywhere = pl.BlockSpec(memory_space=pl.ANY)
    new_shape = jax.ShapeDtypeStruct(stats_old.shape, F32)
    fresh, own, sent = pl.pallas_call(
        functools.partial(step_kernel, pieces=len(pieces), rows=rows, band=band),
        out_shape=(
            new_shape,
            jax.ShapeDtypeStruct((band, order), F32),
            jax.ShapeDtypeStruct((3, band, order), F32),
        ),
        in_specs=[SMEM] + vmem(2 + len(pieces)),
        out_specs=(anywhere, *vmem(2)),
        scratch_shapes=[
            pltpu.VMEM((order, order), BF16),
            pltpu.VMEM(square, F32),
            pltpu.VMEM(square, F32),
            pltpu.VMEM(square, F32),
            pltpu.VMEM(square, BF16),
            pltpu.VMEM(square, BF16),
            pltpu.VMEM(square, BF16),
            pltpu.VMEM((order, order), BF16),
            pltpu.VMEM((2 * band, order), BF16),
            pltpu.VMEM(rows_pair, F32),
            pltpu.SemaphoreType.DMA((2,)),
        ],
        compiler_params=pltpu.CompilerParams(vmem_limit_bytes=32 << 20),
        cost_estimate=pl.CostEstimate(flops=20 * order**3, bytes_accessed=order * order * 16, transcendentals=0),
        name="precondition",
    )(place, damped, stats_old, *pieces)
    sent = swap(sent, CORES)
    return pl.pallas_call(
        finish_kernel,
        out_shape=(new_shape, jax.ShapeDtypeStruct((tiles, band, order), F32)),
        in_specs=[SMEM, anywhere] + vmem(3),
        out_specs=(anywhere, anywhere),
        scratch_shapes=[pltpu.VMEM(rows_pair, F32), pltpu.SemaphoreType.DMA((4,))],
        input_output_aliases={1: 0},
        compiler_params=pltpu.CompilerParams(vmem_limit_bytes=8 << 20),
        cost_estimate=pl.CostEstimate(flops=band * order * 4, bytes_accessed=band * order * 32, transcendentals=0),
        name="finish",
    )(place, fresh, stats_old, own, sent)


def solution(mesh):
    in_specs = (P(("rep", "grp"), None), P(("rep", "grp"), None), P(None, "grp", None))
    out_specs = (P(None, "grp", None), P(None, "grp", None))
    return jax.shard_map(
        on_device, mesh=mesh, in_specs=in_specs, out_specs=out_specs, check_vma=False
    )
```

```python
import functools
import math

import jax
import jax.numpy as jnp
from jax import lax
from jax.experimental import pallas as pl
from jax.experimental.pallas import tpu as pltpu
from jax.sharding import PartitionSpec as P

F32 = jnp.float32
BF16 = jnp.bfloat16
DAMPING = 0.01
TILE = 16
LANES = 128
CORE, LINE, HERE, BESIDE, OWN, SENT, ASKED = range(7)


def swap(array, masks):
    reps, group = lax.axis_size("rep"), lax.axis_size("grp")
    pairs = []
    for rep in range(reps):
        for grp in range(group):
            over, along = masks[grp & 1]
            pairs.append((rep * group + grp, (rep ^ over) * group + (grp ^ along)))
    return lax.ppermute(array, ("rep", "grp"), pairs)


CORES = ((0, 1), (0, 1))


def both(first, second):
    return tuple((a[0] ^ b[0], a[1] ^ b[1]) for a, b in zip(first, second))


def plan(reps, lines, rows):
    over = [(1 << bit, 0) for bit in range(reps.bit_length() - 1)]
    along = [(0, 2 << bit) for bit in range(lines.bit_length() - 1)]
    phases = []
    for kind, bits in (("relay", list(zip(over, over[::-1]))), ("direct", list(zip(along, along)))):
        while bits:
            if len(bits) > 1 and rows // 4 >= TILE:
                phases.append((kind, bits[:2]))
                bits, rows = bits[2:], rows // 4
            elif rows // 2 >= TILE:
                phases.append(("halve", bits[:1]))
                bits, rows = bits[1:], rows // 2
            else:
                phases.append(("add", bits[:1]))
                bits = bits[1:]
    return phases, rows


def position(phases, tile, rep, grp):
    here = jnp.int32(0)
    for kind, bits in phases:
        if kind != "add":
            for masks in bits:
                flags = [jnp.where((rep & over) | (grp & along), 1, 0) for over, along in masks]
                here = here * 2 + jnp.where(tile == 0, flags[0], flags[1])
    return here


def reduce_phase(total, kind, bits, after_all):
    if kind == "add":
        return total + swap(total, bits[0])
    if kind == "halve":
        keep, send = jnp.split(total, 2)
        return keep + swap(send, bits[0])
    keep, second, first, last = jnp.split(total, 4)
    if kind == "relay":
        last = swap(last, bits[0])
        first = swap(first, bits[0])
        second = second + last
        after_all.append(second)
        second = swap(second, bits[1])
        return keep + first + second
    second, first, last = swap(second, bits[1]), swap(first, bits[0]), swap(last, both(*bits))
    return keep + last + first + second


def gather_phase(whole, kind, bits):
    if kind == "add":
        return {0: whole}
    if kind == "halve":
        return {0: whole, 1: swap(whole, bits[0])}
    last, first, second = swap(whole, both(*bits)), swap(whole, bits[0]), swap(whole, bits[1])
    return {0: whole, 2: first, 1: second, 3: last}


def vmem(count):
    return [pl.BlockSpec(memory_space=pltpu.VMEM)] * count


SMEM = pl.BlockSpec(memory_space=pltpu.SMEM)


def dot(a, b, contract=(1, 0)):
    return lax.dot_general(
        a, b, (((contract[0],), (contract[1],)), ((), ())), preferred_element_type=F32
    )


def term_kernel(place, grads, acts, out, *, other, rows):
    order = acts.shape[1]
    columns = pl.ds(pl.multiple_of((place[CORE] ^ other) * order, order), order)
    term = dot(grads[:, columns], acts[...], (0, 0))
    for block in range(order // rows):
        there = pl.ds(pl.multiple_of((block ^ place[BESIDE if other else HERE]) * rows, rows), rows)
        out[there, :] = term[block * rows : (block + 1) * rows]


def gradient_term(place, grads, acts, other, rows):
    tokens, order = acts.shape
    return pl.pallas_call(
        functools.partial(term_kernel, other=other, rows=rows),
        out_shape=jax.ShapeDtypeStruct((order, order), F32),
        in_specs=[SMEM] + vmem(2),
        out_specs=vmem(1)[0],
        compiler_params=pltpu.CompilerParams(vmem_limit_bytes=16 << 20),
        cost_estimate=pl.CostEstimate(
            flops=2 * tokens * order * order, bytes_accessed=4 * tokens * order, transcendentals=0
        ),
        name="gradient_term",
    )(place, grads, acts)


def on_diagonal(rows, columns, start):
    row = lax.broadcasted_iota(jnp.int32, (rows, columns), 0) + start
    return lax.broadcasted_iota(jnp.int32, (rows, columns), 1) == row


def columns_for(digit, lines):
    return [0] + [digit ^ other for other in range(digit + 1, lines)]


def stage_kernel(place, stats, whole, *outs, tiles, lines):
    rows, order = stats.shape[1:]
    width = order // lines
    height = rows + TILE
    diagonal = on_diagonal(rows, order, place[OWN])
    row = lax.broadcasted_iota(jnp.int32, (TILE, order), 0)
    for other in range(2):
        for side in range(2):
            values = stats[(place[ASKED] ^ side) * tiles + (place[CORE] ^ other)]
            high = values.astype(BF16)
            low = (2 * other + side) * height
            whole[low : low + rows, :] = high
            rest = values - high.astype(F32)
            rest = jnp.sum(jnp.where(diagonal, rest, 0.0), axis=0, keepdims=True)
            middle = rest.astype(BF16).astype(F32)
            tail = jnp.where(row == 0, middle, jnp.where(row == 1, rest - middle, 0.0))
            whole[low + rows : low + height, :] = tail.astype(BF16)
    for digit, out in enumerate(outs, 1):
        for index, column in enumerate(columns_for(digit, lines)):
            start = pl.multiple_of((place[LINE] ^ column) * width, width)
            for other in range(2):
                low = 2 * other * height
                values = whole[low : low + height, pl.ds(start, width)]
                out[other * height : (other + 1) * height, index * width : (index + 1) * width] = values


def mirror_kernel(place, whole, received, mine, turned, out, *, rows, lines):
    order = out.shape[2]
    width = order // lines
    height = rows + TILE
    wide = mine.shape[1]
    diagonal = on_diagonal(width, width, 0)

    def at(digit):
        return pl.ds(pl.multiple_of((place[LINE] ^ digit) * width, width), width)

    def rows_of(digit, core):
        start = ((place[LINE] ^ digit) * 2 + (place[CORE] ^ core)) * rows
        return pl.ds(pl.multiple_of(start, rows), rows)

    for index, part in enumerate((mine, turned)):
        side = place[ASKED] ^ index
        low, first = index * height, wide + index * order

        def damp(digit, tails):
            tails = [values.astype(F32) for values in tails]
            vector = sum((values[:1] + values[1:2] for values in tails), jnp.full((1, width), DAMPING, F32))
            out[side, at(digit), at(digit)] += jnp.where(diagonal, vector, 0.0)

        out[side, rows_of(0, 0), :] = whole[low : low + rows, :].astype(F32)
        out[side, rows_of(0, 1), :] = received[:rows, first : first + order].astype(F32)
        for digit in range(1, lines):
            out[side, at(digit), at(0)] = out[side, at(0), at(digit)].T
        lanes = pl.ds(pl.multiple_of(first + place[LINE] * width, width), width)
        damp(0, [whole[low + rows : low + height, at(0)], received[rows:height, lanes]])
        start = 0
        for digit in range(1, lines):
            tails = [part[core * height + rows : (core + 1) * height, start : start + width] for core in range(2)]
            for column in columns_for(digit, lines):
                other = digit ^ column
                for core in range(2):
                    values = part[core * height : core * height + rows, start : start + width]
                    out[side, rows_of(digit, core), at(other)] = values.astype(F32)
                if column:
                    out[side, at(other), at(digit)] = out[side, at(digit), at(other)].T
                start += width
            damp(digit, tails)


def collect_kernel(place, *refs, rows):
    parts, out = refs[:-1], refs[-1]
    order = out.shape[2]
    height = rows + TILE
    for index in range(2):
        side = place[ASKED] ^ index
        vector = jnp.full((1, order), DAMPING, F32)
        for part in parts:
            tail = part[index * height + rows : (index + 1) * height, :].astype(F32)
            vector += tail[:1] + tail[1:2]
        for number, part in enumerate(parts):
            start = ((place[LINE] ^ number // 2) * 2 + (place[CORE] ^ number % 2)) * rows
            start = pl.multiple_of(start, rows)
            values = part[index * height : index * height + rows, :].astype(F32)
            out[side, pl.ds(start, rows), :] = values + jnp.where(on_diagonal(rows, order, start), vector, 0.0)


def step_kernel(place, damped, stats, *refs, numbers, rows, band):
    parts = refs[: len(numbers)]
    fresh, own, sent, grad, gram, scaled, power, factors, offs, seconds, left_root, right_rows, added, sems = refs[len(numbers) :]
    tiles = stats.shape[0] // 2
    order = grad.shape[0]
    for part, blocks in zip(parts, numbers):
        for index, block in enumerate(blocks):
            start = pl.multiple_of((block ^ place[HERE]) * rows, rows)
            grad[pl.ds(start, rows), :] = part[index * rows : (index + 1) * rows, :]
    copies = []
    for side in range(2):
        gram[side] = dot(grad[...], grad[...], (side, side))
        chain = side * tiles + place[CORE]
        added[side] = stats[chain] + gram[side, pl.ds(pl.multiple_of(place[OWN], band), band), :]
        copies.append(pltpu.make_async_copy(added.at[side], fresh.at[chain], sems.at[side]))
        copies[side].start()
        sent[side] = gram[side, pl.ds(pl.multiple_of(place[SENT], band), band), :]
    step = min(order, LANES)
    strips = [slice(low, low + step) for low in range(0, order, step)]
    eye = on_diagonal(step, step, 0)
    sides = range(2)

    def on_eye(block):
        return jnp.where(eye, block, 0.0)

    def beside(block):
        return jnp.sum(on_eye(block), axis=1, keepdims=True)

    def above(ref, side):
        blocks = [jnp.sum(on_eye(ref[side, strip, strip]), axis=0, keepdims=True) for strip in strips]
        return jnp.concatenate(blocks, axis=1)

    def off_eye(ref, side, strip, values):
        ref[side, strip, :] = values.astype(BF16)
        ref[side, strip, strip] = jnp.where(eye, 0.0, values[:, strip]).astype(BF16)

    scales = []
    for side in sides:
        total = jnp.zeros((8, order), F32)
        for strip in strips:
            value = gram[side, strip, :] + damped[side, strip, :]
            scaled[side, strip, :] = value
            total += jnp.sum((value * value).reshape(step // 8, 8, order), axis=0)
        scales.append(2.5 / jnp.sqrt(jnp.sum(total, keepdims=True)))

    def iterate(side, strip):
        return scaled[side, strip, :] * scales[side]

    for side in sides:
        for strip in strips:
            value = iterate(side, strip)
            factors[side, strip, :] = (value * -0.25).astype(BF16)
            block = (jnp.where(eye, 5.0, 0.0) - value[:, strip]) * 0.25
            factors[side, strip, strip] = block.astype(BF16)
    for side in sides:
        square = dot(factors[side], factors[side])
        for strip in strips:
            value = square[strip]
            power[side, strip, :] = value
            power[side, strip, strip] = value[:, strip] - jnp.where(eye, 1.5625, 0.0)
            off_eye(seconds, side, strip, value)
    for side in sides:
        square = dot(seconds[side], seconds[side])
        across = above(power, side) + 3.125
        for strip in strips:
            value = power[side, strip, :]
            down = beside(value[:, strip])
            value = square[strip] + value * (across + down)
            power[side, strip, :] = value
            power[side, strip, strip] = value[:, strip] - on_eye(down * down)
            off_eye(offs, side, strip, value)
            off_eye(seconds, side, strip, iterate(side, strip))
    for side in sides:
        product = dot(seconds[side], offs[side])
        across = above(power, side)
        for strip in strips:
            first, value = iterate(side, strip), power[side, strip, :]
            down = beside(first[:, strip])
            value = product[strip] + first * (across + 2.44140625) + down * value
            offs[side, strip, :] = (value * -0.25).astype(BF16)
            block = jnp.where(eye, 5.0 + down * across[:, strip], 0.0) - value[:, strip]
            offs[side, strip, strip] = (block * 0.25).astype(BF16)
    quarters = [jnp.sqrt(jnp.sqrt(scale)) for scale in scales]
    left_root[...] = (dot(factors[0], offs[0]) * quarters[0]).astype(BF16)
    right_rows[:band] = factors[1, pl.ds(pl.multiple_of(place[OWN], band), band), :]
    right_rows[band:] = factors[1, pl.ds(pl.multiple_of(place[SENT], band), band), :]
    right_root = (dot(right_rows[...], offs[1]) * quarters[1]).astype(BF16)
    inner = dot(right_root, grad[...])
    high = inner.astype(BF16)
    low = (inner - high.astype(F32)).astype(BF16)
    update = (dot(high, left_root[...]) + dot(low, left_root[...])) * math.sqrt(order)
    own[...] = update[:band]
    sent[2] = update[band:]
    for copy in copies:
        copy.wait()


def finish_kernel(place, fresh, stats, own, sent, out, update, added, sems):
    tiles = update.shape[0]
    other = 1 - place[CORE]
    copies = [
        pltpu.make_async_copy(own, update.at[place[CORE]], sems.at[0]),
        pltpu.make_async_copy(sent.at[2], update.at[other], sems.at[1]),
    ]
    for side in range(2):
        chain = side * tiles + other
        added[side] = stats[chain] + sent[side]
        copies.append(pltpu.make_async_copy(added.at[side], out.at[chain], sems.at[2 + side]))
    for copy in copies:
        copy.start()
    for copy in copies:
        copy.wait()


def stage_stats(place, stats_old, tiles, lines):
    band, order = stats_old.shape[1:]
    height, width = band + TILE, order // lines
    outs = [jax.ShapeDtypeStruct((4 * height, order), BF16)]
    for number in range(1, lines if width % LANES == 0 else 1):
        outs.append(jax.ShapeDtypeStruct((2 * height, width * len(columns_for(number, lines))), BF16))
    return pl.pallas_call(
        functools.partial(stage_kernel, tiles=tiles, lines=lines),
        out_shape=tuple(outs),
        in_specs=[SMEM] + vmem(1),
        out_specs=tuple(vmem(len(outs))),
        compiler_params=pltpu.CompilerParams(vmem_limit_bytes=8 << 20),
        cost_estimate=pl.CostEstimate(flops=band * order * 20, bytes_accessed=band * order * 32, transcendentals=0),
        name="stage_stats",
    )(place, stats_old)


def join_kernel(whole, *refs, half):
    parts, out = refs[:-1], refs[-1]
    height = half // 2
    start = 0
    for part in parts:
        out[:, start : start + part.shape[1]] = part[height:, :]
        start += part.shape[1]
    for side in range(2):
        out[:, start : start + whole.shape[1]] = whole[half + side * height : half + (side + 1) * height, :]
        start += whole.shape[1]


def join_stats(whole, stats):
    half, order = whole.shape[0] // 2, whole.shape[1]
    wide = 2 * order + sum(part.shape[1] for part in stats)
    return pl.pallas_call(
        functools.partial(join_kernel, half=half),
        out_shape=jax.ShapeDtypeStruct((half // 2, wide), BF16),
        in_specs=vmem(1 + len(stats)),
        out_specs=vmem(1)[0],
        compiler_params=pltpu.CompilerParams(vmem_limit_bytes=8 << 20),
        cost_estimate=pl.CostEstimate(flops=10**10, bytes_accessed=2 * half * wide, transcendentals=0),
        name="join_stats",
    )(whole, *stats)


def after(array, *others):
    return lax.optimization_barrier((array, *others))[0]


def whole_stats(place, whole, received, stats, lines, order, band):
    half = 2 * (band + TILE)
    if order // lines % LANES == 0:
        kernel = functools.partial(mirror_kernel, rows=band, lines=lines)
        operands = [whole, received, *stats]
    else:
        kernel, operands = functools.partial(collect_kernel, rows=band), []
        for index, part in enumerate((whole, *stats)):
            operands += [part[:half], received[index * half : (index + 1) * half]]
    return pl.pallas_call(
        kernel,
        out_shape=jax.ShapeDtypeStruct((2, order, order), F32),
        in_specs=[SMEM] + vmem(len(operands)),
        out_specs=vmem(1)[0],
        compiler_params=pltpu.CompilerParams(vmem_limit_bytes=16 << 20),
        cost_estimate=pl.CostEstimate(flops=order * order * 8, bytes_accessed=order * order * 12, transcendentals=0),
        name="whole_stats",
    )(place, *operands)


def on_device(activations, out_grads, stats_old):
    order = activations.shape[1]
    tiles = out_grads.shape[1] // order
    band = stats_old.shape[1]
    rep, grp = lax.axis_index("rep"), lax.axis_index("grp")
    reps, lines = lax.axis_size("rep"), lax.axis_size("grp") // 2
    core, line = grp & 1, grp >> 1

    phases, rows = plan(reps, lines, order)
    here, beside = (position(phases, core ^ other, rep, grp) for other in (0, 1))
    place = jnp.stack([core, line, here, beside, grp * band, (grp ^ 1) * band, rep & 1]).astype(jnp.int32)

    sent = swap(gradient_term(place, out_grads, activations, 1, rows), CORES)
    whole, *shares = stage_stats(place, stats_old, tiles, lines)
    place, *shares = lax.optimization_barrier((place, *shares))
    stats = [swap(share, ((0, 2 * step),) * 2) for step, share in enumerate(shares or [whole] * (lines - 1), 1)]
    total = gradient_term(place, out_grads, activations, 0, rows) + sent
    mirrored = order // lines % LANES == 0
    relayed = []
    for index, (kind, bits) in enumerate(phases):
        if index == (reps > 1):
            if mirrored:
                stats = [after(part, *relayed) for part in stats]
                others = join_stats(whole, stats)
                received = swap(others, CORES)
                wide = sum(part.shape[1] for part in stats)
                own = jnp.concatenate([part[: band + TILE] for part in stats], axis=1)
                mine = jnp.concatenate([own, received[:, :wide]], axis=0)
                stats = [mine, swap(mine, ((1, 0), (1, 0)))]
                total, others = lax.optimization_barrier((total, others))
            else:
                half = 2 * (band + TILE)
                received = swap(jnp.concatenate([part[half:] for part in (whole, *stats)], axis=0), CORES)
                total, *stats = lax.optimization_barrier((total, *stats))
        total = reduce_phase(total, kind, bits, relayed)
    pieces, numbers, count = [total.astype(BF16)], [[0]], 1
    for index, (kind, bits) in enumerate(reversed(phases)):
        if index == len(phases) - 1:
            damped = whole_stats(place, whole, received, stats, lines, order, band)
        joined = pieces[0] if len(pieces) == 1 else jnp.concatenate(pieces, axis=0)
        if index == len(phases) - 1 and mirrored:
            joined = after(joined, stats[1])
        inner = sum(numbers, [])
        parts = gather_phase(joined, kind, bits)
        pieces = list(parts.values())
        numbers = [[digit * count + number for number in inner] for digit in parts]
        count *= len(parts)

    rows_pair = (2, band, order)
    square = (2, order, order)
    anywhere = pl.BlockSpec(memory_space=pl.ANY)
    new_shape = jax.ShapeDtypeStruct(stats_old.shape, F32)
    fresh, own, sent = pl.pallas_call(
        functools.partial(step_kernel, numbers=numbers, rows=rows, band=band),
        out_shape=(
            new_shape,
            jax.ShapeDtypeStruct((band, order), F32),
            jax.ShapeDtypeStruct((3, band, order), F32),
        ),
        in_specs=[SMEM] + vmem(2 + len(pieces)),
        out_specs=(anywhere, *vmem(2)),
        scratch_shapes=[
            pltpu.VMEM((order, order), BF16),
            pltpu.VMEM(square, F32),
            pltpu.VMEM(square, F32),
            pltpu.VMEM(square, F32),
            pltpu.VMEM(square, BF16),
            pltpu.VMEM(square, BF16),
            pltpu.VMEM(square, BF16),
            pltpu.VMEM((order, order), BF16),
            pltpu.VMEM((2 * band, order), BF16),
            pltpu.VMEM(rows_pair, F32),
            pltpu.SemaphoreType.DMA((2,)),
        ],
        compiler_params=pltpu.CompilerParams(vmem_limit_bytes=32 << 20),
        cost_estimate=pl.CostEstimate(flops=20 * order**3, bytes_accessed=order * order * 16, transcendentals=0),
        name="precondition",
    )(place, damped, stats_old, *pieces)
    sent = swap(sent, CORES)
    return pl.pallas_call(
        finish_kernel,
        out_shape=(new_shape, jax.ShapeDtypeStruct((tiles, band, order), F32)),
        in_specs=[SMEM, anywhere] + vmem(3),
        out_specs=(anywhere, anywhere),
        scratch_shapes=[pltpu.VMEM(rows_pair, F32), pltpu.SemaphoreType.DMA((4,))],
        input_output_aliases={1: 0},
        compiler_params=pltpu.CompilerParams(vmem_limit_bytes=8 << 20),
        cost_estimate=pl.CostEstimate(flops=band * order * 4, bytes_accessed=band * order * 32, transcendentals=0),
        name="finish",
    )(place, fresh, stats_old, own, sent)


def solution(mesh):
    in_specs = (P(("rep", "grp"), None), P(("rep", "grp"), None), P(None, "grp", None))
    out_specs = (P(None, "grp", None), P(None, "grp", None))
    return jax.shard_map(
        on_device, mesh=mesh, in_specs=in_specs, out_specs=out_specs, check_vma=False
    )
```

```python
import functools
import math

import jax
import jax.numpy as jnp
from jax import lax
from jax.experimental import pallas as pl
from jax.experimental.pallas import tpu as pltpu
from jax.sharding import PartitionSpec as P

F32 = jnp.float32
BF16 = jnp.bfloat16
DAMPING = 0.01
TILE = 16
LANES = 128
CORE, LINE, HERE, BESIDE, OWN, SENT, ASKED = range(7)


def swap(array, masks):
    reps, group = lax.axis_size("rep"), lax.axis_size("grp")
    pairs = []
    for rep in range(reps):
        for grp in range(group):
            over, along = masks[grp & 1]
            pairs.append((rep * group + grp, (rep ^ over) * group + (grp ^ along)))
    return lax.ppermute(array, ("rep", "grp"), pairs)


CORES = ((0, 1), (0, 1))


def both(first, second):
    return tuple((a[0] ^ b[0], a[1] ^ b[1]) for a, b in zip(first, second))


def plan(reps, lines, rows):
    over = [(1 << bit, 0) for bit in range(reps.bit_length() - 1)]
    along = [(0, 2 << bit) for bit in range(lines.bit_length() - 1)]
    phases = []
    for kind, bits in (("relay", list(zip(over, over[::-1]))), ("direct", list(zip(along, along)))):
        while bits:
            if len(bits) > 1 and rows // 4 >= TILE:
                phases.append((kind, bits[:2]))
                bits, rows = bits[2:], rows // 4
            elif rows // 2 >= TILE:
                phases.append(("halve", bits[:1]))
                bits, rows = bits[1:], rows // 2
            else:
                phases.append(("add", bits[:1]))
                bits = bits[1:]
    return phases, rows


def position(phases, tile, rep, grp):
    here = jnp.int32(0)
    for kind, bits in phases:
        if kind != "add":
            for masks in bits:
                flags = [jnp.where((rep & over) | (grp & along), 1, 0) for over, along in masks]
                here = here * 2 + jnp.where(tile == 0, flags[0], flags[1])
    return here


def reduce_phase(total, kind, bits, after_all):
    if kind == "add":
        return total + swap(total, bits[0])
    if kind == "halve":
        keep, send = jnp.split(total, 2)
        return keep + swap(send, bits[0])
    keep, second, first, last = jnp.split(total, 4)
    if kind == "relay":
        last = swap(last, bits[0])
        first = swap(first, bits[0])
        second = second + last
        after_all.append(second)
        second = swap(second, bits[1])
        return keep + first + second
    second, first, last = swap(second, bits[1]), swap(first, bits[0]), swap(last, both(*bits))
    return keep + last + first + second


def gather_phase(whole, kind, bits):
    if kind == "add":
        return {0: whole}
    if kind == "halve":
        return {0: whole, 1: swap(whole, bits[0])}
    last, first, second = swap(whole, both(*bits)), swap(whole, bits[0]), swap(whole, bits[1])
    return {0: whole, 2: first, 1: second, 3: last}


def vmem(count):
    return [pl.BlockSpec(memory_space=pltpu.VMEM)] * count


SMEM = pl.BlockSpec(memory_space=pltpu.SMEM)


def dot(a, b, contract=(1, 0)):
    return lax.dot_general(
        a, b, (((contract[0],), (contract[1],)), ((), ())), preferred_element_type=F32
    )


def term_kernel(place, grads, acts, out, *, other, rows):
    order = acts.shape[1]
    columns = pl.ds(pl.multiple_of((place[CORE] ^ other) * order, order), order)
    term = dot(grads[:, columns], acts[...], (0, 0))
    for block in range(order // rows):
        there = pl.ds(pl.multiple_of((block ^ place[BESIDE if other else HERE]) * rows, rows), rows)
        out[there, :] = term[block * rows : (block + 1) * rows]


def gradient_term(place, grads, acts, other, rows):
    tokens, order = acts.shape
    return pl.pallas_call(
        functools.partial(term_kernel, other=other, rows=rows),
        out_shape=jax.ShapeDtypeStruct((order, order), F32),
        in_specs=[SMEM] + vmem(2),
        out_specs=vmem(1)[0],
        compiler_params=pltpu.CompilerParams(vmem_limit_bytes=16 << 20),
        cost_estimate=pl.CostEstimate(
            flops=2 * tokens * order * order, bytes_accessed=4 * tokens * order, transcendentals=0
        ),
        name="gradient_term",
    )(place, grads, acts)


def on_diagonal(rows, columns, start):
    row = lax.broadcasted_iota(jnp.int32, (rows, columns), 0) + start
    return lax.broadcasted_iota(jnp.int32, (rows, columns), 1) == row


def columns_for(digit, lines):
    return [0] + [digit ^ other for other in range(digit + 1, lines)]


def stage_kernel(place, stats, whole, *outs, tiles, lines):
    rows, order = stats.shape[1:]
    width = order // lines
    height = rows + TILE
    diagonal = on_diagonal(rows, order, place[OWN])
    row = lax.broadcasted_iota(jnp.int32, (TILE, order), 0)
    for other in range(2):
        for side in range(2):
            values = stats[(place[ASKED] ^ side) * tiles + (place[CORE] ^ other)]
            high = values.astype(BF16)
            low = (2 * other + side) * height
            whole[low : low + rows, :] = high
            rest = values - high.astype(F32)
            rest = jnp.sum(jnp.where(diagonal, rest, 0.0), axis=0, keepdims=True)
            middle = rest.astype(BF16).astype(F32)
            tail = jnp.where(row == 0, middle, jnp.where(row == 1, rest - middle, 0.0))
            whole[low + rows : low + height, :] = tail.astype(BF16)
    for digit, out in enumerate(outs, 1):
        for index, column in enumerate(columns_for(digit, lines)):
            start = pl.multiple_of((place[LINE] ^ column) * width, width)
            for other in range(2):
                low = 2 * other * height
                values = whole[low : low + height, pl.ds(start, width)]
                out[other * height : (other + 1) * height, index * width : (index + 1) * width] = values


def mirror_kernel(place, whole, received, mine, turned, out, *, rows, lines):
    order = out.shape[2]
    width = order // lines
    height = rows + TILE
    wide = mine.shape[1]
    diagonal = on_diagonal(width, width, 0)

    def at(digit):
        return pl.ds(pl.multiple_of((place[LINE] ^ digit) * width, width), width)

    def rows_of(digit, core):
        start = ((place[LINE] ^ digit) * 2 + (place[CORE] ^ core)) * rows
        return pl.ds(pl.multiple_of(start, rows), rows)

    for index, part in enumerate((mine, turned)):
        side = place[ASKED] ^ index
        low, first = index * height, wide + index * order

        def damp(digit, tails):
            tails = [values.astype(F32) for values in tails]
            vector = sum((values[:1] + values[1:2] for values in tails), jnp.full((1, width), DAMPING, F32))
            out[side, at(digit), at(digit)] += jnp.where(diagonal, vector, 0.0)

        out[side, rows_of(0, 0), :] = whole[low : low + rows, :].astype(F32)
        out[side, rows_of(0, 1), :] = received[:rows, first : first + order].astype(F32)
        for digit in range(1, lines):
            out[side, at(digit), at(0)] = out[side, at(0), at(digit)].T
        lanes = pl.ds(pl.multiple_of(first + place[LINE] * width, width), width)
        damp(0, [whole[low + rows : low + height, at(0)], received[rows:height, lanes]])
        start = 0
        for digit in range(1, lines):
            tails = [part[core * height + rows : (core + 1) * height, start : start + width] for core in range(2)]
            for column in columns_for(digit, lines):
                other = digit ^ column
                for core in range(2):
                    values = part[core * height : core * height + rows, start : start + width]
                    out[side, rows_of(digit, core), at(other)] = values.astype(F32)
                if column:
                    out[side, at(other), at(digit)] = out[side, at(digit), at(other)].T
                start += width
            damp(digit, tails)


def collect_kernel(place, *refs, rows):
    parts, out = refs[:-1], refs[-1]
    order = out.shape[2]
    height = rows + TILE
    for index in range(2):
        side = place[ASKED] ^ index
        vector = jnp.full((1, order), DAMPING, F32)
        for part in parts:
            tail = part[index * height + rows : (index + 1) * height, :].astype(F32)
            vector += tail[:1] + tail[1:2]
        for number, part in enumerate(parts):
            start = ((place[LINE] ^ number // 2) * 2 + (place[CORE] ^ number % 2)) * rows
            start = pl.multiple_of(start, rows)
            values = part[index * height : index * height + rows, :].astype(F32)
            out[side, pl.ds(start, rows), :] = values + jnp.where(on_diagonal(rows, order, start), vector, 0.0)


def step_kernel(place, damped, stats, *refs, numbers, rows, band):
    parts = refs[: len(numbers)]
    fresh, own, sent, sent_update, grad, gram, scaled, power, factors, offs, seconds, left_root, right_rows, added, sems = refs[len(numbers) :]
    tiles = stats.shape[0] // 2
    order = grad.shape[0]
    for part, blocks in zip(parts, numbers):
        for index, block in enumerate(blocks):
            start = pl.multiple_of((block ^ place[HERE]) * rows, rows)
            grad[pl.ds(start, rows), :] = part[index * rows : (index + 1) * rows, :]
    copies = []
    for side in range(2):
        gram[side] = dot(grad[...], grad[...], (side, side))
        chain = side * tiles + place[CORE]
        added[side] = stats[chain] + gram[side, pl.ds(pl.multiple_of(place[OWN], band), band), :]
        copies.append(pltpu.make_async_copy(added.at[side], fresh.at[chain], sems.at[side]))
        copies[side].start()
        sent[side] = gram[side, pl.ds(pl.multiple_of(place[SENT], band), band), :]
    step = min(order, LANES)
    strips = [slice(low, low + step) for low in range(0, order, step)]
    eye = on_diagonal(step, step, 0)
    sides = range(2)

    def on_eye(block):
        return jnp.where(eye, block, 0.0)

    def beside(block):
        return jnp.sum(on_eye(block), axis=1, keepdims=True)

    def above(ref, side):
        blocks = [jnp.sum(on_eye(ref[side, strip, strip]), axis=0, keepdims=True) for strip in strips]
        return jnp.concatenate(blocks, axis=1)

    def off_eye(ref, side, strip, values):
        ref[side, strip, :] = values.astype(BF16)
        ref[side, strip, strip] = jnp.where(eye, 0.0, values[:, strip]).astype(BF16)

    scales = []
    for side in sides:
        total = jnp.zeros((8, order), F32)
        for strip in strips:
            value = gram[side, strip, :] + damped[side, strip, :]
            scaled[side, strip, :] = value
            total += jnp.sum((value * value).reshape(step // 8, 8, order), axis=0)
        scales.append(2.5 / jnp.sqrt(jnp.sum(total, keepdims=True)))

    def iterate(side, strip):
        return scaled[side, strip, :] * scales[side]

    for side in sides:
        for strip in strips:
            value = iterate(side, strip)
            factors[side, strip, :] = (value * -0.25).astype(BF16)
            block = (jnp.where(eye, 5.0, 0.0) - value[:, strip]) * 0.25
            factors[side, strip, strip] = block.astype(BF16)
    for side in sides:
        square = dot(factors[side], factors[side])
        for strip in strips:
            value = square[strip]
            power[side, strip, :] = value
            power[side, strip, strip] = value[:, strip] - jnp.where(eye, 1.5625, 0.0)
            off_eye(seconds, side, strip, value)
    for side in sides:
        square = dot(seconds[side], seconds[side])
        across = above(power, side) + 3.125
        for strip in strips:
            value = power[side, strip, :]
            down = beside(value[:, strip])
            value = square[strip] + value * (across + down)
            power[side, strip, :] = value
            power[side, strip, strip] = value[:, strip] - on_eye(down * down)
            off_eye(offs, side, strip, value)
            off_eye(seconds, side, strip, iterate(side, strip))
    for side in sides:
        product = dot(seconds[side], offs[side])
        across = above(power, side)
        for strip in strips:
            first, value = iterate(side, strip), power[side, strip, :]
            down = beside(first[:, strip])
            value = product[strip] + first * (across + 2.44140625) + down * value
            offs[side, strip, :] = (value * -0.25).astype(BF16)
            block = jnp.where(eye, 5.0 + down * across[:, strip], 0.0) - value[:, strip]
            offs[side, strip, strip] = (block * 0.25).astype(BF16)
    quarters = [jnp.sqrt(jnp.sqrt(scale)) for scale in scales]
    left_root[...] = (dot(factors[0], offs[0]) * quarters[0]).astype(BF16)
    right_rows[:band] = factors[1, pl.ds(pl.multiple_of(place[OWN], band), band), :]
    right_rows[band:] = factors[1, pl.ds(pl.multiple_of(place[SENT], band), band), :]
    right_root = (dot(right_rows[...], offs[1]) * quarters[1]).astype(BF16)
    inner = dot(right_root, grad[...])
    high = inner.astype(BF16)
    low = (inner - high.astype(F32)).astype(BF16)
    update = (dot(high, left_root[...]) + dot(low, left_root[...])) * math.sqrt(order)
    own[...] = update[:band]
    sent_update[...] = update[band:]
    for copy in copies:
        copy.wait()


def finish_kernel(place, fresh, stats, own, sent, sent_update, out, update, added, sems):
    tiles = update.shape[0]
    other = 1 - place[CORE]
    copies = [
        pltpu.make_async_copy(own, update.at[place[CORE]], sems.at[0]),
        pltpu.make_async_copy(sent_update, update.at[other], sems.at[1]),
    ]
    for side in range(2):
        chain = side * tiles + other
        added[side] = stats[chain] + sent[side]
        copies.append(pltpu.make_async_copy(added.at[side], out.at[chain], sems.at[2 + side]))
    for copy in copies:
        copy.start()
    for copy in copies:
        copy.wait()


def stage_stats(place, stats_old, tiles, lines):
    band, order = stats_old.shape[1:]
    height, width = band + TILE, order // lines
    outs = [jax.ShapeDtypeStruct((4 * height, order), BF16)]
    for number in range(1, lines if width % LANES == 0 else 1):
        outs.append(jax.ShapeDtypeStruct((2 * height, width * len(columns_for(number, lines))), BF16))
    return pl.pallas_call(
        functools.partial(stage_kernel, tiles=tiles, lines=lines),
        out_shape=tuple(outs),
        in_specs=[SMEM] + vmem(1),
        out_specs=tuple(vmem(len(outs))),
        compiler_params=pltpu.CompilerParams(vmem_limit_bytes=8 << 20),
        cost_estimate=pl.CostEstimate(flops=band * order * 20, bytes_accessed=band * order * 32, transcendentals=0),
        name="stage_stats",
    )(place, stats_old)


def join_kernel(whole, *refs, half):
    parts, out = refs[:-1], refs[-1]
    height = half // 2
    start = 0
    for part in parts:
        out[:, start : start + part.shape[1]] = part[height:, :]
        start += part.shape[1]
    for side in range(2):
        out[:, start : start + whole.shape[1]] = whole[half + side * height : half + (side + 1) * height, :]
        start += whole.shape[1]


def join_stats(whole, stats):
    half, order = whole.shape[0] // 2, whole.shape[1]
    wide = 2 * order + sum(part.shape[1] for part in stats)
    return pl.pallas_call(
        functools.partial(join_kernel, half=half),
        out_shape=jax.ShapeDtypeStruct((half // 2, wide), BF16),
        in_specs=vmem(1 + len(stats)),
        out_specs=vmem(1)[0],
        compiler_params=pltpu.CompilerParams(vmem_limit_bytes=8 << 20),
        cost_estimate=pl.CostEstimate(flops=10**10, bytes_accessed=2 * half * wide, transcendentals=0),
        name="join_stats",
    )(whole, *stats)


def after(array, *others):
    return lax.optimization_barrier((array, *others))[0]


def whole_stats(place, whole, received, stats, lines, order, band):
    half = 2 * (band + TILE)
    if order // lines % LANES == 0:
        kernel = functools.partial(mirror_kernel, rows=band, lines=lines)
        operands = [whole, received, *stats]
    else:
        kernel, operands = functools.partial(collect_kernel, rows=band), []
        for index, part in enumerate((whole, *stats)):
            operands += [part[:half], received[index * half : (index + 1) * half]]
    return pl.pallas_call(
        kernel,
        out_shape=jax.ShapeDtypeStruct((2, order, order), F32),
        in_specs=[SMEM] + vmem(len(operands)),
        out_specs=vmem(1)[0],
        compiler_params=pltpu.CompilerParams(vmem_limit_bytes=16 << 20),
        cost_estimate=pl.CostEstimate(flops=order * order * 8, bytes_accessed=order * order * 12, transcendentals=0),
        name="whole_stats",
    )(place, *operands)


def on_device(activations, out_grads, stats_old):
    order = activations.shape[1]
    tiles = out_grads.shape[1] // order
    band = stats_old.shape[1]
    rep, grp = lax.axis_index("rep"), lax.axis_index("grp")
    reps, lines = lax.axis_size("rep"), lax.axis_size("grp") // 2
    core, line = grp & 1, grp >> 1

    phases, rows = plan(reps, lines, order)
    here, beside = (position(phases, core ^ other, rep, grp) for other in (0, 1))
    place = jnp.stack([core, line, here, beside, grp * band, (grp ^ 1) * band, rep & 1]).astype(jnp.int32)

    sent = swap(gradient_term(place, out_grads, activations, 1, rows), CORES)
    whole, *shares = stage_stats(place, stats_old, tiles, lines)
    place, *shares = lax.optimization_barrier((place, *shares))
    stats = [swap(share, ((0, 2 * step),) * 2) for step, share in enumerate(shares or [whole] * (lines - 1), 1)]
    total = gradient_term(place, out_grads, activations, 0, rows) + sent
    mirrored = order // lines % LANES == 0
    relayed = []
    for index, (kind, bits) in enumerate(phases):
        if index == (reps > 1):
            if mirrored:
                stats = [after(part, *relayed) for part in stats]
                others = join_stats(whole, stats)
                received = swap(others, CORES)
                wide = sum(part.shape[1] for part in stats)
                own = jnp.concatenate([part[: band + TILE] for part in stats], axis=1)
                mine = jnp.concatenate([own, received[:, :wide]], axis=0)
                stats = [mine, swap(mine, ((1, 0), (1, 0)))]
                total, others = lax.optimization_barrier((total, others))
            else:
                half = 2 * (band + TILE)
                received = swap(jnp.concatenate([part[half:] for part in (whole, *stats)], axis=0), CORES)
                total, *stats = lax.optimization_barrier((total, *stats))
        total = reduce_phase(total, kind, bits, relayed)
    pieces, numbers, count = [total.astype(BF16)], [[0]], 1
    for index, (kind, bits) in enumerate(reversed(phases)):
        if index == len(phases) - 1:
            damped = whole_stats(place, whole, received, stats, lines, order, band)
        joined = pieces[0] if len(pieces) == 1 else jnp.concatenate(pieces, axis=0)
        if index == len(phases) - 1 and mirrored:
            joined = after(joined, stats[1])
        inner = sum(numbers, [])
        parts = gather_phase(joined, kind, bits)
        pieces = list(parts.values())
        numbers = [[digit * count + number for number in inner] for digit in parts]
        count *= len(parts)

    rows_pair = (2, band, order)
    square = (2, order, order)
    anywhere = pl.BlockSpec(memory_space=pl.ANY)
    new_shape = jax.ShapeDtypeStruct(stats_old.shape, F32)
    fresh, own, sent, sent_update = pl.pallas_call(
        functools.partial(step_kernel, numbers=numbers, rows=rows, band=band),
        out_shape=(
            new_shape,
            jax.ShapeDtypeStruct((band, order), F32),
            jax.ShapeDtypeStruct(rows_pair, F32),
            jax.ShapeDtypeStruct((band, order), F32),
        ),
        in_specs=[SMEM] + vmem(2 + len(pieces)),
        out_specs=(anywhere, *vmem(3)),
        scratch_shapes=[
            pltpu.VMEM((order, order), BF16),
            pltpu.VMEM(square, F32),
            pltpu.VMEM(square, F32),
            pltpu.VMEM(square, F32),
            pltpu.VMEM(square, BF16),
            pltpu.VMEM(square, BF16),
            pltpu.VMEM(square, BF16),
            pltpu.VMEM((order, order), BF16),
            pltpu.VMEM((2 * band, order), BF16),
            pltpu.VMEM(rows_pair, F32),
            pltpu.SemaphoreType.DMA((2,)),
        ],
        compiler_params=pltpu.CompilerParams(vmem_limit_bytes=32 << 20),
        cost_estimate=pl.CostEstimate(flops=20 * order**3, bytes_accessed=order * order * 16, transcendentals=0),
        name="precondition",
    )(place, damped, stats_old, *pieces)
    sent, sent_update = swap(sent, CORES), swap(sent_update, CORES)
    return pl.pallas_call(
        finish_kernel,
        out_shape=(new_shape, jax.ShapeDtypeStruct((tiles, band, order), F32)),
        in_specs=[SMEM, anywhere] + vmem(4),
        out_specs=(anywhere, anywhere),
        scratch_shapes=[pltpu.VMEM(rows_pair, F32), pltpu.SemaphoreType.DMA((4,))],
        input_output_aliases={1: 0},
        compiler_params=pltpu.CompilerParams(vmem_limit_bytes=8 << 20),
        cost_estimate=pl.CostEstimate(flops=band * order * 4, bytes_accessed=band * order * 32, transcendentals=0),
        name="finish",
    )(place, fresh, stats_old, own, sent, sent_update)


def solution(mesh):
    in_specs = (P(("rep", "grp"), None), P(("rep", "grp"), None), P(None, "grp", None))
    out_specs = (P(None, "grp", None), P(None, "grp", None))
    return jax.shard_map(
        on_device, mesh=mesh, in_specs=in_specs, out_specs=out_specs, check_vma=False
    )
```

```python
import functools
import math

import jax
import jax.numpy as jnp
from jax import lax
from jax.experimental import pallas as pl
from jax.experimental.pallas import tpu as pltpu
from jax.sharding import PartitionSpec as P

F32 = jnp.float32
BF16 = jnp.bfloat16
DAMPING = 0.01
TILE = 16
LANES = 128
CORE, LINE, HERE, BESIDE, OWN, SENT, ASKED = range(7)


def swap(array, masks):
    reps, group = lax.axis_size("rep"), lax.axis_size("grp")
    pairs = []
    for rep in range(reps):
        for grp in range(group):
            over, along = masks[grp & 1]
            pairs.append((rep * group + grp, (rep ^ over) * group + (grp ^ along)))
    return lax.ppermute(array, ("rep", "grp"), pairs)


CORES = ((0, 1), (0, 1))


def both(first, second):
    return tuple((a[0] ^ b[0], a[1] ^ b[1]) for a, b in zip(first, second))


def plan(reps, lines, rows):
    over = [(1 << bit, 0) for bit in range(reps.bit_length() - 1)]
    along = [(0, 2 << bit) for bit in range(lines.bit_length() - 1)]
    phases = []
    for kind, bits in (("relay", list(zip(over, over[::-1]))), ("direct", list(zip(along, along)))):
        while bits:
            if len(bits) > 1 and rows // 4 >= TILE:
                phases.append((kind, bits[:2]))
                bits, rows = bits[2:], rows // 4
            elif rows // 2 >= TILE:
                phases.append(("halve", bits[:1]))
                bits, rows = bits[1:], rows // 2
            else:
                phases.append(("add", bits[:1]))
                bits = bits[1:]
    return phases, rows


def position(phases, tile, rep, grp):
    here = jnp.int32(0)
    for kind, bits in phases:
        if kind != "add":
            for masks in bits:
                flags = [jnp.where((rep & over) | (grp & along), 1, 0) for over, along in masks]
                here = here * 2 + jnp.where(tile == 0, flags[0], flags[1])
    return here


def reduce_phase(total, kind, bits, after_all):
    if kind == "add":
        return total + swap(total, bits[0])
    if kind == "halve":
        keep, send = jnp.split(total, 2)
        return keep + swap(send, bits[0])
    keep, second, first, last = jnp.split(total, 4)
    if kind == "relay":
        last = swap(last, bits[0])
        first = swap(first, bits[0])
        second = second + last
        after_all.append(second)
        second = swap(second, bits[1])
        return keep + first + second
    second, first, last = swap(second, bits[1]), swap(first, bits[0]), swap(last, both(*bits))
    return keep + last + first + second


def gather_phase(whole, kind, bits):
    if kind == "add":
        return {0: whole}
    if kind == "halve":
        return {0: whole, 1: swap(whole, bits[0])}
    last, first, second = swap(whole, both(*bits)), swap(whole, bits[0]), swap(whole, bits[1])
    return {0: whole, 2: first, 1: second, 3: last}


def vmem(count):
    return [pl.BlockSpec(memory_space=pltpu.VMEM)] * count


SMEM = pl.BlockSpec(memory_space=pltpu.SMEM)


def dot(a, b, contract=(1, 0)):
    return lax.dot_general(
        a, b, (((contract[0],), (contract[1],)), ((), ())), preferred_element_type=F32
    )


def term_kernel(place, grads, acts, out, *, other, rows):
    order = acts.shape[1]
    columns = pl.ds(pl.multiple_of((place[CORE] ^ other) * order, order), order)
    term = dot(grads[:, columns], acts[...], (0, 0))
    for block in range(order // rows):
        there = pl.ds(pl.multiple_of((block ^ place[BESIDE if other else HERE]) * rows, rows), rows)
        out[there, :] = term[block * rows : (block + 1) * rows]


def gradient_term(place, grads, acts, other, rows):
    tokens, order = acts.shape
    return pl.pallas_call(
        functools.partial(term_kernel, other=other, rows=rows),
        out_shape=jax.ShapeDtypeStruct((order, order), F32),
        in_specs=[SMEM] + vmem(2),
        out_specs=vmem(1)[0],
        compiler_params=pltpu.CompilerParams(vmem_limit_bytes=16 << 20),
        cost_estimate=pl.CostEstimate(
            flops=2 * tokens * order * order, bytes_accessed=4 * tokens * order, transcendentals=0
        ),
        name="gradient_term",
    )(place, grads, acts)


def on_diagonal(rows, columns, start):
    row = lax.broadcasted_iota(jnp.int32, (rows, columns), 0) + start
    return lax.broadcasted_iota(jnp.int32, (rows, columns), 1) == row


def columns_for(digit, lines):
    return [0] + [digit ^ other for other in range(digit + 1, lines)]


def stage_kernel(place, stats, whole, *outs, tiles, lines):
    rows, order = stats.shape[1:]
    width = order // lines
    height = rows + TILE
    diagonal = on_diagonal(rows, order, place[OWN])
    row = lax.broadcasted_iota(jnp.int32, (TILE, order), 0)
    for other in range(2):
        for side in range(2):
            values = stats[(place[ASKED] ^ side) * tiles + (place[CORE] ^ other)]
            high = values.astype(BF16)
            low = (2 * other + side) * height
            whole[low : low + rows, :] = high
            rest = values - high.astype(F32)
            rest = jnp.sum(jnp.where(diagonal, rest, 0.0), axis=0, keepdims=True)
            middle = rest.astype(BF16).astype(F32)
            tail = jnp.where(row == 0, middle, jnp.where(row == 1, rest - middle, 0.0))
            whole[low + rows : low + height, :] = tail.astype(BF16)
    for digit, out in enumerate(outs, 1):
        for index, column in enumerate(columns_for(digit, lines)):
            start = pl.multiple_of((place[LINE] ^ column) * width, width)
            for other in range(2):
                low = 2 * other * height
                values = whole[low : low + height, pl.ds(start, width)]
                out[other * height : (other + 1) * height, index * width : (index + 1) * width] = values


def mirror_kernel(place, whole, received, mine, turned, out, *, rows, lines):
    order = out.shape[2]
    width = order // lines
    height = rows + TILE
    wide = mine.shape[1]
    diagonal = on_diagonal(width, width, 0)

    def at(digit):
        return pl.ds(pl.multiple_of((place[LINE] ^ digit) * width, width), width)

    def rows_of(digit, core):
        start = ((place[LINE] ^ digit) * 2 + (place[CORE] ^ core)) * rows
        return pl.ds(pl.multiple_of(start, rows), rows)

    for index, part in enumerate((mine, turned)):
        side = place[ASKED] ^ index
        low, first = index * height, wide + index * order

        def damp(digit, tails):
            tails = [values.astype(F32) for values in tails]
            vector = sum((values[:1] + values[1:2] for values in tails), jnp.full((1, width), DAMPING, F32))
            out[side, at(digit), at(digit)] += jnp.where(diagonal, vector, 0.0)

        out[side, rows_of(0, 0), :] = whole[low : low + rows, :].astype(F32)
        out[side, rows_of(0, 1), :] = received[:rows, first : first + order].astype(F32)
        for digit in range(1, lines):
            out[side, at(digit), at(0)] = out[side, at(0), at(digit)].T
        lanes = pl.ds(pl.multiple_of(first + place[LINE] * width, width), width)
        damp(0, [whole[low + rows : low + height, at(0)], received[rows:height, lanes]])
        start = 0
        for digit in range(1, lines):
            tails = [part[core * height + rows : (core + 1) * height, start : start + width] for core in range(2)]
            for column in columns_for(digit, lines):
                other = digit ^ column
                for core in range(2):
                    values = part[core * height : core * height + rows, start : start + width]
                    out[side, rows_of(digit, core), at(other)] = values.astype(F32)
                if column:
                    out[side, at(other), at(digit)] = out[side, at(digit), at(other)].T
                start += width
            damp(digit, tails)


def collect_kernel(place, *refs, rows):
    parts, out = refs[:-1], refs[-1]
    order = out.shape[2]
    height = rows + TILE
    for index in range(2):
        side = place[ASKED] ^ index
        vector = jnp.full((1, order), DAMPING, F32)
        for part in parts:
            tail = part[index * height + rows : (index + 1) * height, :].astype(F32)
            vector += tail[:1] + tail[1:2]
        for number, part in enumerate(parts):
            start = ((place[LINE] ^ number // 2) * 2 + (place[CORE] ^ number % 2)) * rows
            start = pl.multiple_of(start, rows)
            values = part[index * height : index * height + rows, :].astype(F32)
            out[side, pl.ds(start, rows), :] = values + jnp.where(on_diagonal(rows, order, start), vector, 0.0)


def step_kernel(place, damped, stats, *refs, numbers, rows, band):
    parts = refs[: len(numbers)]
    fresh, own, sent, sent_update, grad, gram, scaled, power, factors, offs, seconds, left_root, right_rows, added, sems = refs[len(numbers) :]
    tiles = stats.shape[0] // 2
    order = grad.shape[0]
    for part, blocks in zip(parts, numbers):
        for index, block in enumerate(blocks):
            start = pl.multiple_of((block ^ place[HERE]) * rows, rows)
            grad[pl.ds(start, rows), :] = part[index * rows : (index + 1) * rows, :]
    copies = []
    for side in range(2):
        gram[side] = dot(grad[...], grad[...], (side, side))
        chain = side * tiles + place[CORE]
        added[side] = stats[chain] + gram[side, pl.ds(pl.multiple_of(place[OWN], band), band), :]
        copies.append(pltpu.make_async_copy(added.at[side], fresh.at[chain], sems.at[side]))
        copies[side].start()
        sent[side] = gram[side, pl.ds(pl.multiple_of(place[SENT], band), band), :]
    step = min(order, LANES)
    strips = [slice(low, low + step) for low in range(0, order, step)]
    eye = on_diagonal(step, step, 0)
    sides = range(2)

    def on_eye(block):
        return jnp.where(eye, block, 0.0)

    def beside(block):
        return jnp.sum(on_eye(block), axis=1, keepdims=True)

    def above(ref, side):
        blocks = [jnp.sum(on_eye(ref[side, strip, strip]), axis=0, keepdims=True) for strip in strips]
        return jnp.concatenate(blocks, axis=1)

    def off_eye(ref, side, strip, values):
        ref[side, strip, :] = values.astype(BF16)
        ref[side, strip, strip] = jnp.where(eye, 0.0, values[:, strip]).astype(BF16)

    scales = []
    for side in sides:
        total = jnp.zeros((8, order), F32)
        for strip in strips:
            value = gram[side, strip, :] + damped[side, strip, :]
            scaled[side, strip, :] = value
            total += jnp.sum((value * value).reshape(step // 8, 8, order), axis=0)
        scales.append(2.5 / jnp.sqrt(jnp.sum(total, keepdims=True)))

    def iterate(side, strip):
        return scaled[side, strip, :] * scales[side]

    for side in sides:
        for strip in strips:
            value = iterate(side, strip)
            factors[side, strip, :] = (value * -0.25).astype(BF16)
            block = (jnp.where(eye, 5.0, 0.0) - value[:, strip]) * 0.25
            factors[side, strip, strip] = block.astype(BF16)
    for side in sides:
        square = dot(factors[side], factors[side])
        for strip in strips:
            value = square[strip]
            power[side, strip, :] = value
            power[side, strip, strip] = value[:, strip] - jnp.where(eye, 1.5625, 0.0)
            off_eye(seconds, side, strip, value)
    for side in sides:
        square = dot(seconds[side], seconds[side])
        across = above(power, side) + 3.125
        for strip in strips:
            value = power[side, strip, :]
            down = beside(value[:, strip])
            value = square[strip] + value * (across + down)
            power[side, strip, :] = value
            power[side, strip, strip] = value[:, strip] - on_eye(down * down)
            off_eye(offs, side, strip, value)
            off_eye(seconds, side, strip, iterate(side, strip))
    for side in sides:
        product = dot(seconds[side], offs[side])
        across = above(power, side)
        for strip in strips:
            first, value = iterate(side, strip), power[side, strip, :]
            down = beside(first[:, strip])
            value = product[strip] + first * (across + 2.44140625) + down * value
            offs[side, strip, :] = (value * -0.25).astype(BF16)
            block = jnp.where(eye, 5.0 + down * across[:, strip], 0.0) - value[:, strip]
            offs[side, strip, strip] = (block * 0.25).astype(BF16)
    quarters = [jnp.sqrt(jnp.sqrt(scale)) for scale in scales]
    left_root[...] = (dot(factors[0], offs[0]) * quarters[0]).astype(BF16)
    right_rows[:band] = factors[1, pl.ds(pl.multiple_of(place[OWN], band), band), :]
    right_rows[band:] = factors[1, pl.ds(pl.multiple_of(place[SENT], band), band), :]
    right_root = (dot(right_rows[...], offs[1]) * quarters[1]).astype(BF16)
    inner = dot(right_root, grad[...])
    high = inner.astype(BF16)
    low = (inner - high.astype(F32)).astype(BF16)
    update = (dot(high, left_root[...]) + dot(low, left_root[...])) * math.sqrt(order)
    own[...] = update[:band]
    sent_update[...] = update[band:]
    for copy in copies:
        copy.wait()


def finish_kernel(place, fresh, stats, own, sent, sent_update, out, update, added, sems):
    tiles = update.shape[0]
    other = 1 - place[CORE]
    copies = [
        pltpu.make_async_copy(own, update.at[place[CORE]], sems.at[0]),
        pltpu.make_async_copy(sent_update, update.at[other], sems.at[1]),
    ]
    for copy in copies:
        copy.start()
    for side in range(2):
        chain = side * tiles + other
        added[side] = stats[chain] + sent[side]
        copies.append(pltpu.make_async_copy(added.at[side], out.at[chain], sems.at[2 + side]))
        copies[-1].start()
    for copy in copies:
        copy.wait()


def stage_stats(place, stats_old, tiles, lines):
    band, order = stats_old.shape[1:]
    height, width = band + TILE, order // lines
    outs = [jax.ShapeDtypeStruct((4 * height, order), BF16)]
    for number in range(1, lines if width % LANES == 0 else 1):
        outs.append(jax.ShapeDtypeStruct((2 * height, width * len(columns_for(number, lines))), BF16))
    return pl.pallas_call(
        functools.partial(stage_kernel, tiles=tiles, lines=lines),
        out_shape=tuple(outs),
        in_specs=[SMEM] + vmem(1),
        out_specs=tuple(vmem(len(outs))),
        compiler_params=pltpu.CompilerParams(vmem_limit_bytes=8 << 20),
        cost_estimate=pl.CostEstimate(flops=band * order * 20, bytes_accessed=band * order * 32, transcendentals=0),
        name="stage_stats",
    )(place, stats_old)


def join_kernel(whole, *refs, half):
    parts, out = refs[:-1], refs[-1]
    height = half // 2
    start = 0
    for part in parts:
        out[:, start : start + part.shape[1]] = part[height:, :]
        start += part.shape[1]
    for side in range(2):
        out[:, start : start + whole.shape[1]] = whole[half + side * height : half + (side + 1) * height, :]
        start += whole.shape[1]


def join_stats(whole, stats):
    half, order = whole.shape[0] // 2, whole.shape[1]
    wide = 2 * order + sum(part.shape[1] for part in stats)
    return pl.pallas_call(
        functools.partial(join_kernel, half=half),
        out_shape=jax.ShapeDtypeStruct((half // 2, wide), BF16),
        in_specs=vmem(1 + len(stats)),
        out_specs=vmem(1)[0],
        compiler_params=pltpu.CompilerParams(vmem_limit_bytes=8 << 20),
        cost_estimate=pl.CostEstimate(flops=10**10, bytes_accessed=2 * half * wide, transcendentals=0),
        name="join_stats",
    )(whole, *stats)


def after(array, *others):
    return lax.optimization_barrier((array, *others))[0]


def whole_stats(place, whole, received, stats, lines, order, band):
    half = 2 * (band + TILE)
    if order // lines % LANES == 0:
        kernel = functools.partial(mirror_kernel, rows=band, lines=lines)
        operands = [whole, received, *stats]
    else:
        kernel, operands = functools.partial(collect_kernel, rows=band), []
        for index, part in enumerate((whole, *stats)):
            operands += [part[:half], received[index * half : (index + 1) * half]]
    return pl.pallas_call(
        kernel,
        out_shape=jax.ShapeDtypeStruct((2, order, order), F32),
        in_specs=[SMEM] + vmem(len(operands)),
        out_specs=vmem(1)[0],
        compiler_params=pltpu.CompilerParams(vmem_limit_bytes=16 << 20),
        cost_estimate=pl.CostEstimate(flops=order * order * 8, bytes_accessed=order * order * 12, transcendentals=0),
        name="whole_stats",
    )(place, *operands)


def on_device(activations, out_grads, stats_old):
    order = activations.shape[1]
    tiles = out_grads.shape[1] // order
    band = stats_old.shape[1]
    rep, grp = lax.axis_index("rep"), lax.axis_index("grp")
    reps, lines = lax.axis_size("rep"), lax.axis_size("grp") // 2
    core, line = grp & 1, grp >> 1

    phases, rows = plan(reps, lines, order)
    here, beside = (position(phases, core ^ other, rep, grp) for other in (0, 1))
    place = jnp.stack([core, line, here, beside, grp * band, (grp ^ 1) * band, rep & 1]).astype(jnp.int32)

    sent = swap(gradient_term(place, out_grads, activations, 1, rows), CORES)
    whole, *shares = stage_stats(place, stats_old, tiles, lines)
    place, *shares = lax.optimization_barrier((place, *shares))
    stats = [swap(share, ((0, 2 * step),) * 2) for step, share in enumerate(shares or [whole] * (lines - 1), 1)]
    total = gradient_term(place, out_grads, activations, 0, rows) + sent
    mirrored = order // lines % LANES == 0
    relayed = []
    for index, (kind, bits) in enumerate(phases):
        if index == (reps > 1):
            if mirrored:
                stats = [after(part, *relayed) for part in stats]
                others = join_stats(whole, stats)
                received = swap(others, CORES)
                wide = sum(part.shape[1] for part in stats)
                own = jnp.concatenate([part[: band + TILE] for part in stats], axis=1)
                mine = jnp.concatenate([own, received[:, :wide]], axis=0)
                stats = [mine, swap(mine, ((1, 0), (1, 0)))]
                total, others = lax.optimization_barrier((total, others))
            else:
                half = 2 * (band + TILE)
                received = swap(jnp.concatenate([part[half:] for part in (whole, *stats)], axis=0), CORES)
                total, *stats = lax.optimization_barrier((total, *stats))
        total = reduce_phase(total, kind, bits, relayed)
    pieces, numbers, count = [total.astype(BF16)], [[0]], 1
    for index, (kind, bits) in enumerate(reversed(phases)):
        if index == len(phases) - 1:
            damped = whole_stats(place, whole, received, stats, lines, order, band)
        joined = pieces[0] if len(pieces) == 1 else jnp.concatenate(pieces, axis=0)
        if index == len(phases) - 1 and mirrored:
            joined = after(joined, stats[1])
        inner = sum(numbers, [])
        parts = gather_phase(joined, kind, bits)
        pieces = list(parts.values())
        numbers = [[digit * count + number for number in inner] for digit in parts]
        count *= len(parts)

    rows_pair = (2, band, order)
    square = (2, order, order)
    anywhere = pl.BlockSpec(memory_space=pl.ANY)
    new_shape = jax.ShapeDtypeStruct(stats_old.shape, F32)
    fresh, own, sent, sent_update = pl.pallas_call(
        functools.partial(step_kernel, numbers=numbers, rows=rows, band=band),
        out_shape=(
            new_shape,
            jax.ShapeDtypeStruct((band, order), F32),
            jax.ShapeDtypeStruct(rows_pair, F32),
            jax.ShapeDtypeStruct((band, order), F32),
        ),
        in_specs=[SMEM] + vmem(2 + len(pieces)),
        out_specs=(anywhere, *vmem(3)),
        scratch_shapes=[
            pltpu.VMEM((order, order), BF16),
            pltpu.VMEM(square, F32),
            pltpu.VMEM(square, F32),
            pltpu.VMEM(square, F32),
            pltpu.VMEM(square, BF16),
            pltpu.VMEM(square, BF16),
            pltpu.VMEM(square, BF16),
            pltpu.VMEM((order, order), BF16),
            pltpu.VMEM((2 * band, order), BF16),
            pltpu.VMEM(rows_pair, F32),
            pltpu.SemaphoreType.DMA((2,)),
        ],
        compiler_params=pltpu.CompilerParams(vmem_limit_bytes=32 << 20),
        cost_estimate=pl.CostEstimate(flops=20 * order**3, bytes_accessed=order * order * 16, transcendentals=0),
        name="precondition",
    )(place, damped, stats_old, *pieces)
    sent, sent_update = swap(sent, CORES), swap(sent_update, CORES)
    return pl.pallas_call(
        finish_kernel,
        out_shape=(new_shape, jax.ShapeDtypeStruct((tiles, band, order), F32)),
        in_specs=[SMEM, anywhere] + vmem(4),
        out_specs=(anywhere, anywhere),
        scratch_shapes=[pltpu.VMEM(rows_pair, F32), pltpu.SemaphoreType.DMA((4,))],
        input_output_aliases={1: 0},
        compiler_params=pltpu.CompilerParams(vmem_limit_bytes=8 << 20),
        cost_estimate=pl.CostEstimate(flops=band * order * 4, bytes_accessed=band * order * 32, transcendentals=0),
        name="finish",
    )(place, fresh, stats_old, own, sent, sent_update)


def solution(mesh):
    in_specs = (P(("rep", "grp"), None), P(("rep", "grp"), None), P(None, "grp", None))
    out_specs = (P(None, "grp", None), P(None, "grp", None))
    return jax.shard_map(
        on_device, mesh=mesh, in_specs=in_specs, out_specs=out_specs, check_vma=False
    )
```
